256 devices in a mesh: prow: 8 (over y, core), pcol: 32 (over z, x).
Axes of the slice: x: 4, y: 4, z: 8, core: 2. Of those that a mesh axis runs over, the one named last changes fastest.
Arguments:
- matrix: float32 [8192, 32768], P('prow', 'pcol'), may hold values from -6 to 6
- pivot_inv: float32 [8, 128, 128], replicated, may hold values from -0.06 to 0.16, as said below
- pattern: int32 [64, 256], P('prow', 'pcol'), may hold values 0 or 1
Outputs:
- factored: float32 [8192, 32768], P('prow', 'pcol')
The draws below stay inside these ranges and needn't reach their ends.
Inputs may be any that keep to these rules, and one draw needn't show every extreme that they name: `pivot_inv`: each block is a positive diagonal plus off-diagonal entries.
All inputs are finite; a program needn't handle non-finite values. No bound on the sum of `pattern` on one device may be relied on, other than what follows from the above.
Results may differ from the reference program's by a relative error of at most 0.0001.
Values sent between devices are 32-bit elements; how exact they have to be, the bound alone decides.
A program may use at most 128 MiB of HBM per device.

```python
import jax
import jax.numpy as jnp
from jax import lax

BLK = 128
PB = 4
W = 512
STEPS = 2
M = 8192
N = 32768


def draw_pivot_inv(key, part):
    key = jax.random.fold_in(key, 7)
    key_diag, key_off = jax.random.split(key)
    diag_vals = jnp.exp(jax.random.uniform(key_diag, (STEPS * PB, BLK), jnp.float32, jnp.log(0.5), jnp.log(2.0)))
    off_vals = jnp.clip(jax.random.normal(key_off, (STEPS * PB, BLK, BLK), jnp.float32), -4.0, 4.0)
    eye_mat = jnp.eye(BLK, dtype=jnp.float32)
    return (eye_mat[None] * diag_vals[:, :, None] + off_vals / jnp.sqrt(jnp.float32(BLK))) * 0.05


def place_ends(entries, key, low, high):
    longest = entries.shape.index(max(entries.shape))
    spots = []
    for shift in (0, 1):
        where = [jax.random.randint(jax.random.fold_in(key, axis), (), 0, length) for axis, length in enumerate(entries.shape)]
        where[longest] = (where[longest] + shift) % entries.shape[longest]
        spots.append(tuple(where))
    return entries.at[spots[0]].set(low).at[spots[1]].set(high)


def shard_levels(own_key, shape, pieces, least, largest):
    factor_of, own = 1.0, jax.random.fold_in(own_key, 6)
    for position, blocks in pieces:
        heights = jnp.exp(jax.random.uniform(jax.random.fold_in(own, position), (blocks,), jnp.float32, least / len(pieces), largest / len(pieces)))
        factor_of = factor_of * jnp.repeat(heights, shape[position] // blocks).reshape([-1 if axis == position else 1 for axis in range(len(shape))])
    return factor_of


def bell_draw(key, dims, width, most, cuts=(), kind=jnp.bfloat16):
    factor_of = shard_levels(key, dims, cuts, -0.22, 0.18) if cuts else 1.0
    result = jax.random.normal(key, dims, jnp.float32) * width * factor_of
    return jnp.minimum(jnp.maximum(result, -most), most).astype(kind)


def setup_inputs(seed: int = 0) -> dict:
    seeds = jax.random.split(jax.random.key(seed), 4)
    return {
        "matrix": bell_draw(seeds[0], (M, N), 1.0, 6.0, ((0, 8), (1, 32)), jnp.float32),
        "pivot_inv": draw_pivot_inv(jax.random.fold_in(seeds[3], 71), 0),
        "pattern": place_ends((jax.random.randint(seeds[2], (M // BLK, N // BLK), 0, 2) < 1).astype(jnp.int32), jax.random.fold_in(seeds[2], 1), 0, 1),
    }


def reference(matrix, pivot_inv, pattern):
    keep = jnp.repeat(jnp.repeat(pattern.astype(jnp.float32), BLK, axis=0), BLK, axis=1)
    work = matrix * keep
    for step_index in range(STEPS):
        first_col = step_index * W
        past_col = first_col + W
        blocks = pivot_inv[step_index * PB:(step_index + 1) * PB]
        column = work[past_col:, first_col:past_col].reshape(-1, PB, BLK)
        lower = jnp.einsum("rpk,pkj->rpj", column, blocks, precision=lax.Precision.HIGHEST).reshape(-1, W)
        upper = work[first_col:past_col, past_col:]
        update = jnp.dot(lower, upper, precision=lax.Precision.HIGHEST, preferred_element_type=jnp.float32)
        work = work.at[past_col:, past_col:].add(-update * keep[past_col:, past_col:])
        work = work.at[past_col:, first_col:past_col].set(lower)
    return work
```

```python
import functools

import jax
import jax.numpy as jnp
from jax import lax
from jax.experimental import pallas as pl
from jax.experimental.pallas import tpu as pltpu
from jax.sharding import PartitionSpec as P

MESH = pl.DeviceIdType.MESH
B = 128
NX, NY, NZ = 4, 4, 8
TICKS = 16
LAG0 = 13
LAG1 = 18

CHILD = (
    (105276967, 572662304, 201327138, 639633410),
    (1073746192, 1073844624, 29323537, 1073758436),
)
DEPTH = (
    (1515870810, 2995618556, 3456105856),
    (1515870810, 3219398634, 4294960132),
)
ROOT_WAY = (0, 2, 1, 3)


def bit(mask, n):
    low, high = mask & 0xFFFF, mask >> 16
    half = jnp.where(n >= 16, jnp.int32(high), jnp.int32(low))
    return lax.rem(lax.shift_right_logical(half, lax.rem(n, 16)), 2)


def split(value):
    high = value.astype(jnp.bfloat16)
    return high, (value - high.astype(jnp.float32)).astype(jnp.bfloat16)


def dot3(a, b):
    (ah, al), (bh, bl) = a, b
    mul = functools.partial(jnp.dot, preferred_element_type=jnp.float32)
    return mul(ah, bl) + mul(al, bh) + mul(ah, bh)


def at(index, size=B):
    return pl.ds(pl.multiple_of(index * size, size), size)


def kernel(
    a_hbm, pinv, pat, out,
    a, lbuf, ubuf, lhi, llo, uhi, ulo,
    lrecv, urecv, lsend, hsend, usend, uhand, load_sem, out_sem,
):
    p, q = lax.axis_index("prow"), lax.axis_index("pcol")
    y, core = lax.div(p, 2), lax.rem(p, 2)
    z, x = lax.div(q, NX), lax.rem(q, NX)

    load = pltpu.make_async_copy(a_hbm, a, load_sem)
    load.start()

    xp, xm = lax.rem(x + 1, NX), lax.rem(x + NX - 1, NX)
    zp, zm = lax.rem(z + 1, NZ), lax.rem(z + NZ - 1, NZ)
    yp, ym = lax.rem(y + 1, NY), lax.rem(y + NY - 1, NY)
    ways = (z * NX + xp, z * NX + xm, zp * NX + x, zm * NX + x)
    rows = (yp * 2 + core, ym * 2 + core)
    mate = y * 2 + 1 - core

    barrier = pltpu.get_barrier_semaphore()
    greet = [{"prow": mate, "pcol": q}] + [{"prow": r, "pcol": q} for r in rows]
    for w in ways:
        greet += [{"prow": p, "pcol": w}, {"prow": mate, "pcol": w}]
    for device in greet:
        pl.semaphore_signal(barrier, inc=1, device_id=device, device_id_type=MESH)
    pl.semaphore_wait(barrier, len(greet))
    load.wait()

    def send_l(stream, slot, way, first=1, count=None):
        part = slot if count is None else pl.ds(slot, count)
        return pltpu.make_async_remote_copy(
            src_ref=lbuf.at[stream, part],
            dst_ref=lbuf.at[stream, part],
            send_sem=lsend.at[stream, way],
            recv_sem=lrecv.at[stream, slot],
            device_id={"prow": y * 2 + 1, "pcol": ways[way]},
            device_id_type=MESH,
        )

    def hand_l(slot, count=None):
        part = slot if count is None else pl.ds(slot, count)
        return pltpu.make_async_remote_copy(
            src_ref=lbuf.at[0, part],
            dst_ref=lbuf.at[0, part],
            send_sem=hsend,
            recv_sem=lrecv.at[0, slot],
            device_id={"prow": mate, "pcol": q},
            device_id_type=MESH,
        )

    def send_u(slot, way, count=None):
        part = slot if count is None else pl.ds(slot, count)
        return pltpu.make_async_remote_copy(
            src_ref=ubuf.at[part],
            dst_ref=ubuf.at[part],
            send_sem=usend.at[way],
            recv_sem=urecv.at[slot],
            device_id={"prow": rows[way], "pcol": q},
            device_id_type=MESH,
        )

    def hand_u(slot, count=None):
        part = slot if count is None else pl.ds(slot, count)
        return pltpu.make_async_remote_copy(
            src_ref=ubuf.at[part],
            dst_ref=ubuf.at[part],
            send_sem=uhand,
            recv_sem=urecv.at[slot],
            device_id={"prow": mate, "pcol": q},
            device_id_type=MESH,
        )

    def wait_l(stream, slot):
        send_l(stream, slot, 0).wait_recv()

    def wait_u(slot):
        send_u(slot, 0).wait_recv()

    def slot_l(i, t, stream):
        if stream == 1:
            return 4 * i + t
        return jnp.where(y == 0, t * 8 + 4 + i, 4 * i + t)

    def slot_u(tick, way, h):
        j = 2 * tick + h
        return jnp.where(
            q == 0, (2 * way + h) * 8 + 4 + tick, lax.div(j, 4) * 8 + 4 * way + lax.rem(j, 4)
        )

    def mask_all():
        def body(n, _):
            i, j = lax.div(n, 8), lax.rem(n, 8)
            a[at(i), at(j)] = a[at(i), at(j)] * pat[i, j].astype(jnp.float32)
            return 0

        lax.fori_loop(0, 64, body, 0)

    def write_out():
        copy = pltpu.make_async_copy(a, out, out_sem)
        copy.start()
        copy.wait()

    def relay_u(tick, way):
        for h in (0, 1):
            slot = slot_u(tick, way, h)
            wait_u(slot)
            on = y < NY - 1 if way == 0 else y > 1
            pl.when(on)(lambda: send_u(slot, way).start())
            hand_u(slot).start()

    def relay_u_step(k, ticks):
        for way in (0, 1):
            tick = k - 3 * (y if way == 0 else NY - y)
            pl.when((tick >= 0) & (tick < ticks))(lambda: relay_u(tick, way))

    def end_relay_u(ticks):
        pl.when(y < NY - 1)(lambda: send_u(0, 0, 2 * ticks).wait_send())
        pl.when(y > 1)(lambda: send_u(0, 1, 2 * ticks).wait_send())
        hand_u(0, 4 * ticks).wait_send()

    def split_l(stream, pair):
        def body(i, _):
            for h in (0, 1):
                hi, lo = split(lbuf[stream, (2 * pair + h) * 8 + i])
                lhi[at(i), h * B : (h + 1) * B] = hi
                llo[at(i), h * B : (h + 1) * B] = lo
            return 0

        lax.fori_loop(0, 8, body, 0)

    def split_u(pair):
        def body(j, _):
            for h in (0, 1):
                hi, lo = split(ubuf[(2 * pair + h) * 8 + j])
                uhi[h * B : (h + 1) * B, at(j)] = hi
                ulo[h * B : (h + 1) * B, at(j)] = lo
            return 0

        lax.fori_loop(0, 8, body, 0)

    def out_tile(tile):
        return pltpu.make_async_copy(a.at[:, at(tile, 256)], out.at[:, at(tile, 256)], out_sem)

    def piece(n, stream):
        pair, tile = lax.div(n, 4), lax.rem(n, 4)

        @pl.when(tile == 0)
        def _():
            def body(i, _):
                if stream == 0:
                    wait_l(0, pair * 16 + i)
                else:
                    wait_u(pair * 16 + i)
                return 0

            lax.fori_loop(0, 16, body, 0)
            split_l(stream, pair)
            split_u(pair)

        cols = at(tile, 256)
        right = (uhi[0:256, cols], ulo[0:256, cols])

        def rows_body(r, _):
            part = at(r, 256)
            a[part, cols] -= dot3((lhi[part, 0:256], llo[part, 0:256]), right)
            return 0

        lax.fori_loop(0, 4, rows_body, 0)

        @pl.when(pair == 3)
        def _():
            def body(i, _):
                for h in (0, 1):
                    c = at(2 * tile + h)
                    a[at(i), c] = a[at(i), c] * pat[i, 2 * tile + h].astype(jnp.float32)
                return 0

            lax.fori_loop(0, 8, body, 0)
            out_tile(tile).start()

    def end_tiles():
        pltpu.make_async_copy(a, out, out_sem).wait()

    def general0():
        def body(k, _):
            relay_u_step(k, TICKS)
            n = k - LAG0
            pl.when(n >= 0)(lambda: piece(n, 0))
            return 0

        lax.fori_loop(0, LAG0 + 16, body, 0)
        end_relay_u(TICKS)
        end_tiles()

    def general1():
        node = q
        mirror = lax.rem(NZ - z, NZ) * NX + lax.rem(NX - x, NX)
        sends, depths = [], []
        for t in range(4):
            n = node if t < 2 else mirror
            tree = t % 2
            flip = 0 if t < 2 else 1
            sends.append([bit(CHILD[tree][w ^ flip], n) for w in range(4)])
            depths.append(sum(bit(DEPTH[tree][b], n) * (1 << b) for b in range(3)))

        def relay(i, t):
            def one(stream):
                slot = slot_l(i, t, stream)
                wait_l(stream, slot)
                for w in range(4):
                    pl.when(sends[t][w] == 1)(lambda: send_l(stream, slot, w).start())
                if stream == 0:
                    hand_l(slot).start()

            pl.when((y > 0) | (i < 4))(lambda: one(0))
            one(1)

        def body(k, _):
            for t in range(4):
                i = k - 2 * depths[t]
                pl.when((i >= 0) & (i < TICKS))(lambda: relay(i, t))
            n = k - LAG1
            pl.when(n >= 0)(lambda: piece(n, 1))
            return 0

        lax.fori_loop(0, LAG1 + 16, body, 0)
        for w in range(4):
            any_way = sum(sends[t][w] for t in range(4))

            @pl.when(any_way > 0)
            def _():
                send_l(1, 0, w, count=TICKS).wait_send()
                pl.when(y > 0)(lambda: send_l(0, 0, w, count=TICKS).wait_send())
                pl.when(y == 0)(lambda: send_l(0, 0, w, count=4).wait_send())

        pl.when(y > 0)(lambda: hand_l(0, count=64).wait_send())
        pl.when(y == 0)(lambda: hand_l(0, count=16).wait_send())
        end_tiles()

    def upper_root():
        mask_all()
        for kb in range(4):
            def body(j, _):
                ubuf[kb * 8 + j] = a[kb * B : (kb + 1) * B, at(j)]
                return 0

            lax.fori_loop(0, 8, body, 0)
            for j in range(4):
                for way in (0, 1):
                    slot = kb * 8 + 4 * way + j
                    send_u(slot, way).start()
                    hand_u(slot).start()
        def body(j, _):
            for kb in range(4):
                hi, lo = split(a[kb * B : (kb + 1) * B, at(j)])
                uhi[kb * B : (kb + 1) * B, at(j)] = hi
                ulo[kb * B : (kb + 1) * B, at(j)] = lo
            return 0

        lax.fori_loop(0, 8, body, 0)

        def step(i, _):
            for t in range(4):
                wait_l(0, t * 8 + 4 + i)
                hi, lo = split(lbuf[0, t * 8 + 4 + i])
                lhi[0:B, t * B : (t + 1) * B] = hi
                llo[0:B, t * B : (t + 1) * B] = lo
            r = at(4 + i)

            def tile_body(tile, _):
                c = at(tile, 256)
                prod = dot3((lhi[0:B, :], llo[0:B, :]), (uhi[:, c], ulo[:, c]))
                for h in (0, 1):
                    j = 2 * tile + h
                    keep = pat[4 + i, j].astype(jnp.float32)
                    block = a[r, at(j)] - prod[:, h * B : (h + 1) * B] * keep
                    a[r, at(j)] = block
                    ubuf[(4 + i) * 8 + j] = block
                return 0

            lax.fori_loop(0, 4, tile_body, 0)
            for j in range(4):
                for way in (0, 1):
                    slot = (4 + i) * 8 + 4 * way + j
                    send_u(slot, way).start()
                    hand_u(slot).start()
            return 0

        lax.fori_loop(0, 4, step, 0)
        write_out()
        for way in (0, 1):
            send_u(0, way, 32).wait_send()
        hand_u(0, 64).wait_send()

    def corner():
        mask_all()
        for kb in range(4):
            for j in range(4):
                ubuf[kb * 8 + 4 + j] = a[kb * B : (kb + 1) * B, (4 + j) * B : (5 + j) * B]
        for tick in range(4):
            for h in (0, 1):
                for way in (0, 1):
                    slot = (2 * way + h) * 8 + 4 + tick
                    send_u(slot, way).start()
                    hand_u(slot).start()
        for kb in range(4):
            c = slice(kb * B, (kb + 1) * B)
            low = dot3(split(a[512:1024, c]), split(pinv[kb]))
            a[512:1024, c] = low
            lhi[512:1024, c], llo[512:1024, c] = split(low)
            for i in range(4):
                lbuf[0, kb * 8 + 4 + i] = low[i * B : (i + 1) * B]
        for i in range(4):
            for t in range(4):
                send_l(0, t * 8 + 4 + i, ROOT_WAY[t]).start()
        for j in range(4):
            c = slice((4 + j) * B, (5 + j) * B)
            prod = dot3((lhi[512:1024, :], llo[512:1024, :]), split(a[0:512, c]))
            for i in range(4):
                r = slice((4 + i) * B, (5 + i) * B)
                keep = pat[4 + i, 4 + j].astype(jnp.float32)
                a[r, c] = a[r, c] - prod[i * B : (i + 1) * B] * keep
        write_out()
        for way in (0, 1):
            send_u(0, way, 8).wait_send()
        hand_u(0, 16).wait_send()
        for t in range(4):
            send_l(0, 0, t, count=4).wait_send()

    def lower_root(stream):
        mask_all()

        def send_block_column(kb):
            for i in range(2):
                for t in range(4):
                    slot = kb * 8 + 4 * i + t
                    send_l(stream, slot, ROOT_WAY[t]).start()

        def first(kb, _):
            c = at(kb)
            right = split(pinv[kb])

            def rows_body(r, _):
                part = at(r, 256)
                low = dot3(split(a[part, c]), right)
                a[part, c] = low
                lhi[part, c], llo[part, c] = split(low)
                for h in (0, 1):
                    lbuf[stream, kb * 8 + 2 * r + h] = low[h * B : (h + 1) * B]
                return 0

            lax.fori_loop(0, 4, rows_body, 0)
            send_block_column(kb)
            return 0

        lax.fori_loop(0, 4, first, 0)

        def second(j):
            c = at(4 + j)
            if stream == 1:
                for kb in range(4):
                    wait_u(kb * 8 + 4 + j)
            for kb in range(4):
                hi, lo = split(ubuf[kb * 8 + 4 + j])
                uhi[kb * B : (kb + 1) * B, 0:B] = hi
                ulo[kb * B : (kb + 1) * B, 0:B] = lo
            inverse = split(pinv[4 + j])

            def rows_body(r, _):
                part = at(r, 256)
                prod = dot3((lhi[part, :], llo[part, :]), (uhi[:, 0:B], ulo[:, 0:B]))
                for h in (0, 1):
                    rb = 2 * r + h
                    keep = pat[rb, 4 + j].astype(jnp.float32)
                    a[at(rb), c] = a[at(rb), c] - prod[h * B : (h + 1) * B] * keep
                low = dot3(split(a[part, c]), inverse)
                a[part, c] = low
                for h in (0, 1):
                    lbuf[stream, (4 + j) * 8 + 2 * r + h] = low[h * B : (h + 1) * B]
                return 0

            lax.fori_loop(0, 4, rows_body, 0)
            send_block_column(4 + j)

        if stream == 0:
            def body(k, _):
                relay_u_step(k, 4)
                pl.when(k >= 10)(lambda: second(k - 10))
                return 0

            lax.fori_loop(0, 14, body, 0)
        else:
            def body(j, _):
                second(j)
                return 0

            lax.fori_loop(0, 4, body, 0)
        write_out()
        if stream == 0:
            end_relay_u(4)
        for t in range(4):
            send_l(stream, 0, t, count=TICKS).wait_send()

    pl.when((q == 0) & (p == 0))(corner)
    pl.when((q == 0) & (core == 0) & (p > 0))(lambda: lower_root(0))
    pl.when((q == 0) & (core == 1))(lambda: lower_root(1))
    pl.when((q > 0) & (p == 0))(upper_root)
    pl.when((q > 0) & (core == 0) & (p > 0))(general0)
    pl.when((q > 0) & (core == 1))(general1)


def shards(matrix, pivot_inv, pattern):
    f32, bf16 = jnp.float32, jnp.bfloat16
    return pl.pallas_call(
        kernel,
        out_shape=jax.ShapeDtypeStruct(matrix.shape, f32),
        in_specs=[
            pl.BlockSpec(memory_space=pl.ANY),
            pl.BlockSpec(memory_space=pltpu.VMEM),
            pl.BlockSpec(memory_space=pltpu.SMEM),
        ],
        out_specs=pl.BlockSpec(memory_space=pl.ANY),
        scratch_shapes=[
            pltpu.VMEM((1024, 1024), f32),
            pltpu.VMEM((2, 64, B, B), f32),
            pltpu.VMEM((64, B, B), f32),
            pltpu.VMEM((1024, 512), bf16),
            pltpu.VMEM((1024, 512), bf16),
            pltpu.VMEM((512, 1024), bf16),
            pltpu.VMEM((512, 1024), bf16),
            pltpu.SemaphoreType.DMA((2, 64)),
            pltpu.SemaphoreType.DMA((64,)),
            pltpu.SemaphoreType.DMA((2, 4)),
            pltpu.SemaphoreType.DMA,
            pltpu.SemaphoreType.DMA((2,)),
            pltpu.SemaphoreType.DMA,
            pltpu.SemaphoreType.DMA,
            pltpu.SemaphoreType.DMA,
        ],
        compiler_params=pltpu.CompilerParams(
            collective_id=0, has_side_effects=True, vmem_limit_bytes=48 << 20
        ),
        cost_estimate=pl.CostEstimate(
            flops=6 * 1024**3, bytes_accessed=8 << 20, transcendentals=0
        ),
        name="factor",
    )(matrix, pivot_inv, pattern)


def solution(mesh):
    return jax.shard_map(
        shards,
        mesh=mesh,
        in_specs=(P("prow", "pcol"), P(), P("prow", "pcol")),
        out_specs=P("prow", "pcol"),
        check_vma=False,
    )
```

```python
import functools

import jax
import jax.numpy as jnp
from jax import lax
from jax.experimental import pallas as pl
from jax.experimental.pallas import tpu as pltpu
from jax.sharding import PartitionSpec as P

MESH = pl.DeviceIdType.MESH
B = 128
NX, NY, NZ = 4, 4, 8
R = 2
TICKS_L = 16 * R
TICKS_U = 16

CHILD = (
    (105276967, 572662304, 201327138, 639633410),
    (1073746192, 1073844624, 29323537, 1073758436),
)
DEPTH = (
    (1515870810, 2995618556, 3456105856),
    (1515870810, 3219398634, 4294960132),
)
ROOT_WAY = (0, 2, 1, 3)


def bit(mask, n):
    low, high = mask & 0xFFFF, mask >> 16
    half = jnp.where(n >= 16, jnp.int32(high), jnp.int32(low))
    return lax.rem(lax.shift_right_logical(half, lax.rem(n, 16)), 2)


def lag(depth):
    return {1: 3, 2: 4, 4: 7}[R] * depth


def split(value):
    high = value.astype(jnp.bfloat16)
    return high, (value - high.astype(jnp.float32)).astype(jnp.bfloat16)


def dot3(a, b):
    (ah, al), (bh, bl) = a, b
    mul = functools.partial(jnp.dot, preferred_element_type=jnp.float32)
    return mul(ah, bl) + mul(al, bh) + mul(ah, bh)


def at(index, size=B):
    return pl.ds(pl.multiple_of(index * size, size), size)


def loop(count, body):
    def step(i, _):
        body(i)
        return 0

    lax.fori_loop(0, count, step, 0)


def kernel(
    a_hbm, pinv_hbm, pat_hbm, a, lhi, llo, uhi, ulo,
    lbuf, ubuf, pinv, pat,
    lrecv, crecv, hrecv, urecv, lsend, csend, hsend, usend, uhand, load_sems,
):
    p, q = lax.axis_index("prow"), lax.axis_index("pcol")
    y, core = lax.div(p, 2), lax.rem(p, 2)
    z, x = lax.div(q, NX), lax.rem(q, NX)
    is_root = (q == 0) | (p == 0)

    load = pltpu.make_async_copy(a_hbm, a, load_sems.at[0])
    load_pat = pltpu.make_async_copy(pat_hbm, pat, load_sems.at[1])
    load_pinv = pltpu.make_async_copy(pinv_hbm, pinv, load_sems.at[2])
    load.start()
    load_pat.start()
    pl.when(is_root)(load_pinv.start)

    xp, xm = lax.rem(x + 1, NX), lax.rem(x + NX - 1, NX)
    zp, zm = lax.rem(z + 1, NZ), lax.rem(z + NZ - 1, NZ)
    yp, ym = lax.rem(y + 1, NY), lax.rem(y + NY - 1, NY)
    ways = (z * NX + xp, z * NX + xm, zp * NX + x, zm * NX + x)
    rows = (yp * 2 + core, ym * 2 + core)
    mate = y * 2 + 1 - core

    barrier = pltpu.get_barrier_semaphore()
    greet = [{"prow": mate, "pcol": q}] + [{"prow": r, "pcol": q} for r in rows]
    for w in ways:
        greet += [{"prow": p, "pcol": w}, {"prow": mate, "pcol": w}]
    for device in greet:
        pl.semaphore_signal(barrier, inc=1, device_id=device, device_id_type=MESH)
    pl.semaphore_wait(barrier, len(greet))
    load.wait()
    load_pat.wait()
    pl.when(is_root)(load_pinv.wait)

    def part(index, count):
        return index if count is None else pl.ds(index, count)

    def copy_l(ref, send_sem, recv_sem, row, pcol):
        return pltpu.make_async_remote_copy(
            src_ref=ref,
            dst_ref=ref,
            send_sem=send_sem,
            recv_sem=recv_sem,
            device_id={"prow": row, "pcol": pcol},
            device_id_type=MESH,
        )

    def send_l(chunk, way, both, count=None):
        chunks = part(chunk, count)
        ref = lbuf.at[chunks] if both else lbuf.at[chunks, 1]
        return copy_l(ref, lsend.at[way], lrecv.at[chunk], y * 2 + 1, ways[way])

    def send_c(chunk, way, count=None):
        ref = lbuf.at[part(chunk, count), 0]
        return copy_l(ref, csend.at[way], crecv.at[chunk], y * 2 + 1, ways[way])

    def hand_l(slot, count=1):
        ref = lbuf.at[pl.ds(slot * R, count * R), 0]
        return copy_l(ref, hsend, hrecv.at[slot], mate, q)

    def send_u(slot, way, count=None):
        return pltpu.make_async_remote_copy(
            src_ref=ubuf.at[part(slot, count)],
            dst_ref=ubuf.at[part(slot, count)],
            send_sem=usend.at[way],
            recv_sem=urecv.at[slot],
            device_id={"prow": rows[way], "pcol": q},
            device_id_type=MESH,
        )

    def hand_u(slot, count=None):
        return pltpu.make_async_remote_copy(
            src_ref=ubuf.at[part(slot, count)],
            dst_ref=ubuf.at[part(slot, count)],
            send_sem=uhand,
            recv_sem=urecv.at[slot],
            device_id={"prow": mate, "pcol": q},
            device_id_type=MESH,
        )

    def wait_u(slot):
        send_u(slot, 0).wait_recv()

    def keep(i, j):
        return pat[i, j].astype(jnp.float32)

    def put_l(stream, slot, block):
        for h in range(R):
            lbuf[slot * R + h, stream] = block[h * (B // R) : (h + 1) * (B // R)]

    def split_block(stream, slot, row, column):
        for h in range(R):
            hi, lo = split(lbuf[slot * R + h, stream])
            into = pl.ds(pl.multiple_of(row * B + h * (B // R), B // R), B // R)
            lhi[into, column * B : (column + 1) * B] = hi
            llo[into, column * B : (column + 1) * B] = lo

    used, tree_of, depth_of = [jnp.int32(0)] * 4, [jnp.int32(0)] * 4, [jnp.int32(0)] * 4
    depths = []
    for t in range(4):
        n = q if t < 2 else lax.rem(NZ - z, NZ) * NX + lax.rem(NX - x, NX)
        tree, flip = t % 2, 0 if t < 2 else 1
        depths.append(sum(bit(DEPTH[tree][b], n) * (1 << b) for b in range(3)))
        for w in range(4):
            has = bit(CHILD[tree][w ^ flip], n)
            used[w] = used[w] + has
            tree_of[w] = tree_of[w] + has * t
            depth_of[w] = depth_of[w] + has * depths[t]
    deepest = jnp.maximum(functools.reduce(jnp.maximum, depths), 5)

    def ready(pair, stream):
        if stream == 0:
            loop(16, lambda i: hand_l(pair * 16 + i).wait_recv())
        else:
            loop(16, lambda i: wait_u(pair * 16 + i))

        def split_both(i):
            for h in (0, 1):
                slot = (2 * pair + h) * 8 + i
                split_block(stream, slot, i, h)
                hi, lo = split(ubuf[slot])
                uhi[h * B : (h + 1) * B, at(i)] = hi
                ulo[h * B : (h + 1) * B, at(i)] = lo

        loop(8, split_both)

    def piece(n, stream):
        pair, tile = lax.div(n, 4), lax.rem(n, 4)
        pl.when(tile == 0)(lambda: ready(pair, stream))

        @pl.when(pair < 3)
        def _():
            cols = at(tile, 256)
            a[:, cols] -= dot3(
                (lhi[:, 0:256], llo[:, 0:256]), (uhi[0:256, cols], ulo[0:256, cols])
            )

    def general0():
        start = 2 * deepest + 3

        def relay(tick, way):
            for h in (0, 1):
                j = 2 * tick + h
                slot = lax.div(j, 4) * 8 + 4 * way + lax.rem(j, 4)
                wait_u(slot)
                on = y < NY - 1 if way == 0 else y > 1
                pl.when(on)(lambda: send_u(slot, way).start())
                hand_u(slot).start()

        def step(k):
            for way in (0, 1):
                tick = k - 3 * (y if way == 0 else NY - y)
                pl.when((tick >= 0) & (tick < TICKS_U))(lambda: relay(tick, way))
            n = k - start
            pl.when(n >= 0)(lambda: piece(n, 0))

        loop(start + 13, step)
        pl.when(y < NY - 1)(lambda: send_u(0, 0, 32).wait_send())
        pl.when(y > 1)(lambda: send_u(0, 1, 32).wait_send())
        hand_u(0, 64).wait_send()

    def general1(both):
        start = lag(deepest) + 4 * R + (0 if both else 4 * R)
        ticks = TICKS_L + (0 if both else 4 * R)

        def chunk_of(i, t):
            return lax.div(i, R) * (4 * R) + t * R + lax.rem(i, R)

        def hand_block(i, t):
            pl.when(lax.rem(i, R) == R - 1)(lambda: hand_l(4 * lax.div(i, R) + t).start())

        def receive(i, t):
            if both:
                send_l(chunk_of(i, t), 0, True).wait_recv()
                hand_block(i, t)
                return

            @pl.when(i < 4 * R)
            def _():
                send_c(chunk_of(i, t), 0).wait_recv()
                hand_block(i, t)

            @pl.when(i >= 4 * R)
            def _():
                send_l(chunk_of(i - 4 * R, t), 0, False).wait_recv()

        def forward(i, way):
            t = tree_of[way]
            if both:
                send_l(chunk_of(i, t), way, True).start()
                return
            pl.when(i < 4 * R)(lambda: send_c(chunk_of(i, t), way).start())
            pl.when(i >= 4 * R)(lambda: send_l(chunk_of(i - 4 * R, t), way, False).start())

        def step(k):
            for t in range(4):
                i = k - lag(depths[t])
                pl.when((i >= 0) & (i < ticks))(lambda: receive(i, t))
            for way in range(4):
                i = k - lag(depth_of[way])
                pl.when((used[way] == 1) & (i >= 0) & (i < ticks))(lambda: forward(i, way))
            n = k - start
            pl.when((n >= 0) & (lax.rem(n, R) == 0))(lambda: piece(lax.div(n, R), 1))

        loop(start + 12 * R + 1, step)
        for way in range(4):

            @pl.when(used[way] == 1)
            def _():
                send_l(0, way, both, TICKS_L).wait_send()
                if not both:
                    send_c(0, way, 4 * R).wait_send()

        hand_l(0, 64 if both else 16).wait_send()

    def mask_block(i, j):
        block = a[at(i), at(j)] * keep(i, j)
        a[at(i), at(j)] = block
        return block

    def upper_root():
        def send_row(kb):
            for j in range(4):
                for way in (0, 1):
                    slot = kb * 8 + 4 * way + j
                    send_u(slot, way).start()
                    hand_u(slot).start()

        def first(kb):
            def body(j):
                ubuf[kb * 8 + j] = mask_block(kb, j)

            loop(8, body)
            send_row(kb)

        loop(4, first)
        for kb in range(4):
            r = slice(kb * B, (kb + 1) * B)
            uhi[r, :], ulo[r, :] = split(dot3(split(pinv[kb]), split(a[r, :])))

        def second(i):
            for t in range(4):
                hand_l(4 * i + t).wait_recv()
                split_block(0, 4 * i + t, 0, t)
            prod = dot3((lhi[0:B, :], llo[0:B, :]), (uhi[...], ulo[...]))
            for j in range(8):
                c = slice(j * B, (j + 1) * B)
                block = (a[at(4 + i), c] - prod[:, c]) * keep(4 + i, j)
                a[at(4 + i), c] = block
                ubuf[(4 + i) * 8 + j] = block
            send_row(4 + i)

        loop(4, second)
        for way in (0, 1):
            send_u(0, way, 32).wait_send()
        hand_u(0, 64).wait_send()

    def corner():
        def start(i):
            for t in range(4):
                put_l(0, 4 * i + t, mask_block(4 + i, t))
            for h in range(R):
                for t in range(4):
                    send_c((4 * i + t) * R + h, ROOT_WAY[t]).start()
            for kb in range(4):
                slot = kb * 8 + 4 + i
                ubuf[slot] = mask_block(kb, 4 + i)
                send_u(slot, 0).start()
                send_u(slot, 1).start()
                hand_u(slot).start()

        loop(4, start)

        def rest(i):
            for j in range(4):
                mask_block(i, j)

        loop(4, rest)
        for kb in range(4):
            c = slice(kb * B, (kb + 1) * B)
            low = dot3(split(a[512:1024, c]), split(pinv[kb]))
            a[512:1024, c] = low
            lhi[512:1024, c], llo[512:1024, c] = split(low)
        for j in range(4):
            c = slice((4 + j) * B, (5 + j) * B)
            prod = dot3((lhi[512:1024, :], llo[512:1024, :]), split(a[0:512, c]))
            for i in range(4):
                r = slice((4 + i) * B, (5 + i) * B)
                a[r, c] = (a[r, c] - prod[i * B : (i + 1) * B]) * keep(4 + i, 4 + j)
        for way in (0, 1):
            send_u(0, way, 16).wait_send()
        hand_u(0, 16).wait_send()
        for way in range(4):
            send_c(0, way, 4 * R).wait_send()

    def lower_root(stream, both):
        def send_column(kb):
            if stream == 0:
                hand_l(kb * 8, 8).start()
                return
            if both:
                hand_l(kb * 8, 8).wait_recv()
            for i in range(2):
                for h in range(R):
                    for t in range(4):
                        chunk = (kb * 8 + 4 * i + t) * R + h
                        send_l(chunk, ROOT_WAY[t], both).start()

        def put_column(kb, low):
            a[:, at(kb)] = low
            for i in range(8):
                put_l(stream, kb * 8 + i, low[i * B : (i + 1) * B])
            send_column(kb)

        def first(kb):
            loop(8, lambda i: mask_block(i, kb))
            low = dot3(split(a[:, at(kb)]), split(pinv[kb]))
            put_column(kb, low)
            for b in range(4):
                c = slice(b * B, (b + 1) * B)

                @pl.when(kb == b)
                def _():
                    lhi[:, c], llo[:, c] = split(a[:, c])

        loop(4, first)

        def second(j):
            for kb in range(4):
                slot = kb * 8 + 4 + j
                wait_u(slot)
                if stream == 0:
                    hand_u(slot).start()
                    pl.when((y == 1) if kb < 2 else (y == 3))(
                        lambda: send_u(slot, 0 if kb < 2 else 1).start()
                    )
            for kb in range(4):
                r = slice(kb * B, (kb + 1) * B)
                uhi[r, 0:B], ulo[r, 0:B] = split(ubuf[kb * 8 + 4 + j])
            c = at(4 + j)
            prod = dot3((lhi[...], llo[...]), (uhi[:, 0:B], ulo[:, 0:B]))
            for i in range(8):
                r = slice(i * B, (i + 1) * B)
                a[r, c] = (a[r, c] - prod[r]) * keep(i, 4 + j)
            put_column(4 + j, dot3(split(a[:, c]), split(pinv[4 + j])))

        loop(4, second)
        if stream == 0:
            hand_u(0, 16).wait_send()
            pl.when(y == 1)(lambda: send_u(0, 0, 8).wait_send())
            pl.when(y == 3)(lambda: send_u(0, 1, 8).wait_send())
            hand_l(0, 64).wait_send()
        else:
            for way in range(4):
                send_l(0, way, both, TICKS_L).wait_send()

    pl.when((q == 0) & (p == 0))(corner)
    pl.when((q == 0) & (core == 0) & (p > 0))(lambda: lower_root(0, True))
    pl.when((q == 0) & (p == 1))(lambda: lower_root(1, False))
    pl.when((q == 0) & (core == 1) & (p > 1))(lambda: lower_root(1, True))
    pl.when((q > 0) & (p == 0))(upper_root)
    pl.when((q > 0) & (core == 0) & (p > 0))(general0)
    pl.when((q > 0) & (p == 1))(lambda: general1(False))
    pl.when((q > 0) & (core == 1) & (p > 1))(lambda: general1(True))


def finish(a, lhi, llo, uhi, ulo, pat_hbm, out, tiles, pat, pat_sem, out_sems):
    general = (lax.axis_index("prow") > 0) & (lax.axis_index("pcol") > 0)

    @pl.when(general)
    def _():
        load = pltpu.make_async_copy(pat_hbm, pat, pat_sem)
        load.start()
        copies = []
        for tile in range(4):
            cols = slice(tile * 256, (tile + 1) * 256)
            right = (uhi[0:256, cols], ulo[0:256, cols])
            tiles[tile] = a[:, cols] - dot3((lhi[:, 0:256], llo[:, 0:256]), right)
            if tile == 0:
                load.wait()
            for i in range(8):
                for h in (0, 1):
                    r, c = slice(i * B, (i + 1) * B), slice(h * B, (h + 1) * B)
                    keep = pat[i, 2 * tile + h].astype(jnp.float32)
                    tiles[tile, r, c] = tiles[tile, r, c] * keep
            copies.append(
                pltpu.make_async_copy(tiles.at[tile], out.at[:, cols], out_sems.at[tile])
            )
            copies[-1].start()
        for copy in copies:
            copy.wait()

    @pl.when(jnp.logical_not(general))
    def _():
        copy = pltpu.make_async_copy(a, out, out_sems.at[0])
        copy.start()
        copy.wait()


def shards(matrix, pivot_inv, pattern):
    f32, bf16 = jnp.float32, jnp.bfloat16
    in_hbm, in_vmem = pl.BlockSpec(memory_space=pltpu.HBM), pl.BlockSpec(memory_space=pltpu.VMEM)
    parts = pl.pallas_call(
        kernel,
        out_shape=[pltpu.VMEM(matrix.shape, f32)]
        + [pltpu.VMEM((1024, 512), bf16)] * 2
        + [pltpu.VMEM((512, 1024), bf16)] * 2,
        in_specs=[in_hbm] * 3,
        out_specs=[in_vmem] * 5,
        scratch_shapes=[
            pltpu.VMEM((64 * R, 2, B // R, B), f32),
            pltpu.VMEM((64, B, B), f32),
            pltpu.VMEM(pivot_inv.shape, f32),
            pltpu.SMEM(pattern.shape, jnp.int32),
            pltpu.SemaphoreType.DMA((64 * R,)),
            pltpu.SemaphoreType.DMA((16 * R,)),
            pltpu.SemaphoreType.DMA((64,)),
            pltpu.SemaphoreType.DMA((64,)),
            pltpu.SemaphoreType.DMA((4,)),
            pltpu.SemaphoreType.DMA((4,)),
            pltpu.SemaphoreType.DMA,
            pltpu.SemaphoreType.DMA((2,)),
            pltpu.SemaphoreType.DMA,
            pltpu.SemaphoreType.DMA((3,)),
        ],
        compiler_params=pltpu.CompilerParams(
            collective_id=0, has_side_effects=True, vmem_limit_bytes=50 << 20
        ),
        cost_estimate=pl.CostEstimate(
            flops=5 * 1024**3, bytes_accessed=8 << 20, transcendentals=0
        ),
        name="factor",
    )(matrix, pivot_inv, pattern)
    return pl.pallas_call(
        finish,
        out_shape=jax.ShapeDtypeStruct(matrix.shape, f32),
        in_specs=[in_vmem] * 5 + [in_hbm],
        out_specs=in_hbm,
        scratch_shapes=[
            pltpu.VMEM((4, 1024, 256), f32),
            pltpu.SMEM(pattern.shape, jnp.int32),
            pltpu.SemaphoreType.DMA,
            pltpu.SemaphoreType.DMA((4,)),
        ],
        compiler_params=pltpu.CompilerParams(vmem_limit_bytes=12 << 20),
        cost_estimate=pl.CostEstimate(
            flops=3 * 512 * 1024**2, bytes_accessed=8 << 20, transcendentals=0
        ),
        name="finish",
    )(*parts, pattern)


def solution(mesh):
    return jax.shard_map(
        shards,
        mesh=mesh,
        in_specs=(P("prow", "pcol"), P(), P("prow", "pcol")),
        out_specs=P("prow", "pcol"),
        check_vma=False,
    )
```

```python
import functools

import jax
import jax.numpy as jnp
from jax import lax
from jax.experimental import pallas as pl
from jax.experimental.pallas import tpu as pltpu
from jax.sharding import PartitionSpec as P

MESH = pl.DeviceIdType.MESH
B = 128
NX, NY, NZ = 4, 4, 8
R = 2
TICKS_L = 16 * R
LAG_U = 5

CHILD = (
    (105276967, 572662304, 201327138, 639633410),
    (1073746192, 1073844624, 29323537, 1073758436),
)
DEPTH = (
    (1515870810, 2995618556, 3456105856),
    (1515870810, 3219398634, 4294960132),
)
ROOT_WAY = (0, 2, 1, 3)


def bit(mask, n):
    low, high = mask & 0xFFFF, mask >> 16
    half = jnp.where(n >= 16, jnp.int32(high), jnp.int32(low))
    return lax.rem(lax.shift_right_logical(half, lax.rem(n, 16)), 2)


def lag(depth):
    return {2: 4, 4: 8}[R] * depth


def split(value):
    high = value.astype(jnp.bfloat16)
    return high, (value - high.astype(jnp.float32)).astype(jnp.bfloat16)


def dot3(a, b):
    (ah, al), (bh, bl) = a, b
    mul = functools.partial(jnp.dot, preferred_element_type=jnp.float32)
    return mul(ah, bl) + mul(al, bh) + mul(ah, bh)


def at(index, size=B):
    return pl.ds(pl.multiple_of(index * size, size), size)


def loop(count, body):
    def step(i, _):
        body(i)
        return 0

    lax.fori_loop(0, count, step, 0)


def kernel(
    a_hbm, pinv_hbm, pat_hbm, a, lhi, llo, uhi, ulo,
    lbuf, ubuf, pinv, pat,
    lrecv, crecv, hrecv, urecv, lsend, csend, hsend, usend, uhand, load_sems,
):
    p, q = lax.axis_index("prow"), lax.axis_index("pcol")
    y, core = lax.div(p, 2), lax.rem(p, 2)
    z, x = lax.div(q, NX), lax.rem(q, NX)
    is_root = (q == 0) | (p == 0)

    xp, xm = lax.rem(x + 1, NX), lax.rem(x + NX - 1, NX)
    zp, zm = lax.rem(z + 1, NZ), lax.rem(z + NZ - 1, NZ)
    yp, ym = lax.rem(y + 1, NY), lax.rem(y + NY - 1, NY)
    ways = (z * NX + xp, z * NX + xm, zp * NX + x, zm * NX + x)
    rows = (yp * 2 + core, ym * 2 + core)
    mate = y * 2 + 1 - core

    barrier = pltpu.get_barrier_semaphore()
    greet = [{"prow": mate, "pcol": q}] + [{"prow": r, "pcol": q} for r in rows]
    for w in ways:
        greet += [{"prow": p, "pcol": w}, {"prow": mate, "pcol": w}]
    for device in greet:
        pl.semaphore_signal(barrier, inc=1, device_id=device, device_id_type=MESH)

    load_pat = pltpu.make_async_copy(pat_hbm, pat, load_sems.at[8])
    load_pinv = pltpu.make_async_copy(pinv_hbm, pinv, load_sems.at[9])
    loads = [
        pltpu.make_async_copy(a_hbm.at[at(i)], a.at[at(i)], load_sems.at[i]) for i in range(8)
    ]
    load_pat.start()
    pl.when(is_root)(load_pinv.start)
    for load in loads:
        load.start()

    def part(index, count):
        return index if count is None else pl.ds(index, count)

    def copy_l(ref, send_sem, recv_sem, row, pcol):
        return pltpu.make_async_remote_copy(
            src_ref=ref,
            dst_ref=ref,
            send_sem=send_sem,
            recv_sem=recv_sem,
            device_id={"prow": row, "pcol": pcol},
            device_id_type=MESH,
        )

    def send_l(tick, t, way, both, count=None):
        ref = lbuf.at[part(tick, count), t]
        if not both:
            ref = lbuf.at[part(tick, count), t, 1]
        return copy_l(ref, lsend.at[way], lrecv.at[4 * tick + t], y * 2 + 1, ways[way])

    def root_l(stream, tick, t, count=None):
        ref = lbuf.at[part(tick, count), t, stream]
        way = ROOT_WAY[t]
        return copy_l(ref, lsend.at[way], lrecv.at[4 * tick + t], y * 2 + 1, ways[way])

    def send_c(tick, t, way, count=None):
        ref = lbuf.at[part(tick, count), t, 0]
        return copy_l(ref, csend.at[way], crecv.at[4 * tick + t], y * 2 + 1, ways[way])

    def hand_l(tick, t, count=2):
        ref = lbuf.at[pl.ds(tick, count), t, 0]
        return copy_l(ref, hsend, hrecv.at[4 * tick + t], mate, q)

    def hand_ticks(tick, count):
        ref = lbuf.at[pl.ds(tick, count), :, 0]
        return copy_l(ref, hsend, hrecv.at[4 * tick], mate, q)

    def copy_u(ref, send_sem, slot, row):
        return pltpu.make_async_remote_copy(
            src_ref=ref,
            dst_ref=ref,
            send_sem=send_sem,
            recv_sem=urecv.at[slot],
            device_id={"prow": row, "pcol": q},
            device_id_type=MESH,
        )

    def send_u(slot, half, way):
        return copy_u(ubuf.at[slot, half], usend.at[way], 2 * slot + half, rows[way])

    def hand_u(slot, half):
        return copy_u(ubuf.at[slot, half], uhand, 2 * slot + half, mate)

    def end_u(sem, blocks):
        copy_u(ubuf.at[pl.ds(0, blocks)], sem, 0, mate).wait_send()

    def start_u(slot, ways_out):
        for half in (0, 1):
            for way in ways_out:
                send_u(slot, half, way).start()
            hand_u(slot, half).start()

    def wait_u(slot):
        for half in (0, 1):
            hand_u(slot, half).wait_recv()

    def put_u(slot, block):
        ubuf[slot] = block.reshape(2, B // 2, B)

    def get_u(slot):
        return ubuf[slot].reshape(B, B)

    def keep(i, j):
        return pat[i, j].astype(jnp.float32)

    def put_l(stream, block_tick, t, block):
        for h in range(R):
            rows_of = slice(h * (B // R), (h + 1) * (B // R))
            lbuf[block_tick * R + h, t, stream] = block[rows_of]

    def split_block(stream, block_tick, t, row, column):
        for h in range(R):
            hi, lo = split(lbuf[block_tick * R + h, t, stream])
            into = pl.ds(pl.multiple_of(row * B + h * (B // R), B // R), B // R)
            lhi[into, column * B : (column + 1) * B] = hi
            llo[into, column * B : (column + 1) * B] = lo

    used, tree_of, depth_of = [jnp.int32(0)] * 4, [jnp.int32(0)] * 4, [jnp.int32(0)] * 4
    first_of, leaf = [jnp.int32(0)] * 4, [jnp.int32(1)] * 4
    depths = []
    for t in range(4):
        n = q if t < 2 else lax.rem(NZ - z, NZ) * NX + lax.rem(NX - x, NX)
        tree, flip = t % 2, 0 if t < 2 else 1
        depths.append(sum(bit(DEPTH[tree][b], n) * (1 << b) for b in range(3)))
        for w in range(4):
            has = bit(CHILD[tree][w ^ flip], n)
            first_of[w] = jnp.where((has == 1) & (leaf[t] == 1), 1, first_of[w])
            leaf[t] = jnp.where(has == 1, 0, leaf[t])
            used[w] = used[w] + has
            tree_of[w] = tree_of[w] + has * t
            depth_of[w] = depth_of[w] + has * depths[t]
    deepest = jnp.maximum(functools.reduce(jnp.maximum, depths), 5)

    def ready(pair, stream):
        if stream == 0:

            def wait_tick(i):
                for t in range(4):
                    hand_l(pair * 4 * R + 2 * i, t).wait_recv()

            loop(2 * R, wait_tick)
        else:
            loop(16, lambda i: wait_u(pair * 16 + i))

        def split_both(i):
            for h in (0, 1):
                for half in (0, 1):
                    split_block(stream, 4 * pair + 2 * h + half, i, 4 * half + i, h)
                    j = 4 * half + i
                    hi, lo = split(get_u((2 * pair + h) * 8 + j))
                    uhi[h * B : (h + 1) * B, at(j)] = hi
                    ulo[h * B : (h + 1) * B, at(j)] = lo

        loop(4, split_both)

    def piece(n, stream):
        pair = lax.shift_right_logical(n, 2)
        tile = n - 4 * pair
        pl.when(tile == 0)(lambda: ready(pair, stream))

        @pl.when(pair < 3)
        def _():
            cols = at(tile, 256)
            a[:, cols] -= dot3(
                (lhi[:, 0:256], llo[:, 0:256]), (uhi[0:256, cols], ulo[0:256, cols])
            )

    def general0():
        start = 4 * deepest + 6

        def relay(tick, way):
            row = lax.shift_right_logical(tick, 2)
            slot = 4 * row + 4 * way + tick
            for half in (0, 1):
                hand_u(slot, half).wait_recv()
                on = y < NY - 1 if way == 0 else y > 1
                pl.when(on)(lambda: send_u(slot, half, way).start())
                hand_u(slot, half).start()

        def step(kk):
            for odd in (0, 1):
                for way in (0, 1):
                    tick = 2 * kk + odd - LAG_U * (y if way == 0 else NY - y)
                    pl.when((tick >= 0) & (tick < 32))(lambda: relay(tick, way))
            n = 2 * kk - start
            pl.when(n >= 0)(lambda: piece(lax.shift_right_logical(n, 1), 0))

        loop(lax.shift_right_logical(start, 1) + 13, step)
        pl.when(y < NY - 1)(lambda: end_u(usend.at[0], 32))
        pl.when(y > 1)(lambda: end_u(usend.at[1], 32))
        end_u(uhand, 64)

    def general1(both):
        start = lag(deepest) + 4 * R + (0 if both else 4 * R)
        ticks = TICKS_L + (0 if both else 4 * R)

        def receive(i, t, odd):
            def hand():
                if odd:
                    hand_l(i - 1, t).start()

            if both:
                send_l(i, t, 0, True).wait_recv()
                hand()
                return

            @pl.when(i < 4 * R)
            def _():
                send_c(i, t, 0).wait_recv()
                hand()

            pl.when(i >= 4 * R)(lambda: send_l(i - 4 * R, t, 0, False).wait_recv())

        def forward(i, way):
            t = tree_of[way]
            if both:
                send_l(i, t, way, True).start()
                return
            pl.when(i < 4 * R)(lambda: send_c(i, t, way).start())
            pl.when(i >= 4 * R)(lambda: send_l(i - 4 * R, t, way, False).start())

        last = [jnp.where(used[way] == 1, ticks, 0) for way in range(4)]
        last_leaf = [jnp.where(leaf[t] == 1, ticks, 0) for t in range(4)]
        lags = [lag(d) for d in depths]
        lags_out = [lag(d) for d in depth_of]

        def relay(k, odd):
            for way in range(4):
                i = k - lags_out[way]

                @pl.when((i >= 0) & (i < last[way]))
                def _():
                    pl.when(first_of[way] == 1)(lambda: receive(i, tree_of[way], odd))
                    forward(i, way)

            for t in range(4):
                i = k - lags[t]
                pl.when((i >= 0) & (i < last_leaf[t]))(lambda: receive(i, t, odd))

        def step(kk):
            relay(2 * kk, False)
            relay(2 * kk + 1, True)
            n = 2 * kk - start
            if R == 2:
                pl.when(n >= 0)(lambda: piece(lax.shift_right_logical(n, 1), 1))
            else:
                even = (n & 2) == 0
                pl.when((n >= 0) & even)(lambda: piece(lax.shift_right_logical(n, 2), 1))

        loop(lax.shift_right_logical(start + 12 * R, 1) + 1, step)
        for way in range(4):

            @pl.when(used[way] == 1)
            def _():
                send_l(0, 0, way, both, TICKS_L).wait_send()
                if not both:
                    send_c(0, 0, way, 4 * R).wait_send()

        hand_ticks(0, TICKS_L if both else 4 * R).wait_send()

    def mask_block(i, j):
        block = a[at(i), at(j)] * keep(i, j)
        a[at(i), at(j)] = block
        return block

    def send_row(kb):
        for j in range(4):
            for half in (0, 1):
                for way in (0, 1):
                    slot = kb * 8 + 4 * way + j
                    send_u(slot, half, way).start()
                    hand_u(slot, half).start()

    def prepare_upper():
        def body(j):
            for kb in range(4):
                put_u(kb * 8 + j, mask_block(kb, j))

        loop(8, body)

    def upper_root():
        loop(4, send_row)
        for kb in range(4):
            r = slice(kb * B, (kb + 1) * B)
            uhi[r, :], ulo[r, :] = split(dot3(split(pinv[kb]), split(a[r, :])))

        def second(i):
            for t in range(4):
                for h in range(0, R, 2):
                    hand_l(i * R + h, t).wait_recv()
                split_block(0, i, t, 0, t)
            prod = dot3((lhi[0:B, :], llo[0:B, :]), (uhi[...], ulo[...]))
            for j in range(8):
                c = slice(j * B, (j + 1) * B)
                block = (a[at(4 + i), c] - prod[:, c]) * keep(4 + i, j)
                a[at(4 + i), c] = block
                put_u((4 + i) * 8 + j, block)
            send_row(4 + i)

        loop(4, second)
        for way in (0, 1):
            end_u(usend.at[way], 32)
        end_u(uhand, 64)

    def prepare_corner():
        def body(i):
            for t in range(4):
                put_l(0, i, t, mask_block(4 + i, t))
                put_u(t * 8 + 4 + i, mask_block(t, 4 + i))

        loop(4, body)

    def corner():
        def start(i):
            for h in range(R):
                for t in range(4):
                    send_c(i * R + h, t, ROOT_WAY[t]).start()
            for kb in range(4):
                for half in (0, 1):
                    for way in (0, 1):
                        send_u(kb * 8 + 4 + i, half, way).start()

        loop(4, start)
        for way in range(4):
            send_c(0, 0, way, 4 * R).wait_send()

        def hand(i):
            for kb in range(4):
                for half in (0, 1):
                    hand_u(kb * 8 + 4 + i, half).start()

        loop(4, hand)

        def rest(i):
            for j in range(4):
                mask_block(i, j)

        loop(4, rest)
        for kb in range(4):
            c = slice(kb * B, (kb + 1) * B)
            low = dot3(split(a[512:1024, c]), split(pinv[kb]))
            a[512:1024, c] = low
            lhi[512:1024, c], llo[512:1024, c] = split(low)
        for j in range(4):
            c = slice((4 + j) * B, (5 + j) * B)
            prod = dot3((lhi[512:1024, :], llo[512:1024, :]), split(a[0:512, c]))
            for i in range(4):
                r = slice((4 + i) * B, (5 + i) * B)
                a[r, c] = (a[r, c] - prod[i * B : (i + 1) * B]) * keep(4 + i, 4 + j)
        for way in (0, 1):
            end_u(usend.at[way], 16)
        end_u(uhand, 16)

    def put_column(stream, kb, low):
        a[:, at(kb)] = low
        for i in range(8):
            put_l(stream, 2 * kb + i // 4, i % 4, low[i * B : (i + 1) * B])

    def lower_first(stream, kb):
        loop(8, lambda i: mask_block(i, kb))
        put_column(stream, kb, dot3(split(a[:, at(kb)]), split(pinv[kb])))

    def lower_root(stream, both):
        def send_column(kb):
            for i in range(2 * R):
                for t in range(4):
                    root_l(stream, kb * 2 * R + i, t).start()

        if not both:
            for kb in range(4):
                wait_u(kb * 8 + 4)
        send_column(0)

        def first(kb):
            lower_first(stream, kb + 1)
            send_column(kb + 1)

        loop(3, first)
        lhi[...], llo[...] = split(a[:, 0:512])

        def second(j):
            def arrive():
                for kb in range(4):
                    slot = kb * 8 + 4 + j
                    for half in (0, 1):
                        hand_u(slot, half).wait_recv()
                        if stream == 0:
                            pl.when((y == 1) if kb < 2 else (y == 3))(
                                lambda: send_u(slot, half, 0 if kb < 2 else 1).start()
                            )
                            hand_u(slot, half).start()

            if both:
                arrive()
            else:
                pl.when(j > 0)(arrive)
            for kb in range(4):
                r = slice(kb * B, (kb + 1) * B)
                uhi[r, 0:B], ulo[r, 0:B] = split(get_u(kb * 8 + 4 + j))
            c = at(4 + j)
            prod = dot3((lhi[...], llo[...]), (uhi[:, 0:B], ulo[:, 0:B]))
            for i in range(8):
                r = slice(i * B, (i + 1) * B)
                a[r, c] = (a[r, c] - prod[r]) * keep(i, 4 + j)
            put_column(stream, 4 + j, dot3(split(a[:, c]), split(pinv[4 + j])))
            send_column(4 + j)

        loop(4, second)
        if stream == 0:
            end_u(uhand, 16)
            pl.when(y == 1)(lambda: end_u(usend.at[0], 8))
            pl.when(y == 3)(lambda: end_u(usend.at[1], 8))
        for t in range(4):
            root_l(stream, 0, t, TICKS_L).wait_send()

    is_corner, is_upper = (q == 0) & (p == 0), (q > 0) & (p == 0)
    lower0, lower1 = (q == 0) & (core == 0) & (p > 0), (q == 0) & (core == 1)
    for load in loads:
        load.wait()
    load_pat.wait()
    pl.when(is_root)(load_pinv.wait)
    pl.when(is_corner)(prepare_corner)
    pl.when(is_upper)(prepare_upper)
    pl.when(lower0)(lambda: lower_first(0, 0))
    pl.when(lower1)(lambda: lower_first(1, 0))
    pl.semaphore_wait(barrier, len(greet))

    pl.when(is_corner)(corner)
    pl.when(is_upper)(upper_root)
    pl.when(lower0)(lambda: lower_root(0, True))
    pl.when(lower1 & (p == 1))(lambda: lower_root(1, False))
    pl.when(lower1 & (p > 1))(lambda: lower_root(1, True))
    pl.when((q > 0) & (core == 0) & (p > 0))(general0)
    pl.when((q > 0) & (p == 1))(lambda: general1(False))
    pl.when((q > 0) & (core == 1) & (p > 1))(lambda: general1(True))


def finish(a, lhi, llo, uhi, ulo, pat_hbm, out, tiles, pat, pat_sem, out_sems):
    general = (lax.axis_index("prow") > 0) & (lax.axis_index("pcol") > 0)

    @pl.when(general)
    def _():
        load = pltpu.make_async_copy(pat_hbm, pat, pat_sem)
        load.start()
        copies = []
        for tile in range(4):
            cols = slice(tile * 256, (tile + 1) * 256)
            right = (uhi[0:256, cols], ulo[0:256, cols])
            tiles[tile] = a[:, cols] - dot3((lhi[:, 0:256], llo[:, 0:256]), right)
            if tile == 0:
                load.wait()
            for i in range(8):
                for h in (0, 1):
                    r, c = slice(i * B, (i + 1) * B), slice(h * B, (h + 1) * B)
                    keep = pat[i, 2 * tile + h].astype(jnp.float32)
                    tiles[tile, r, c] = tiles[tile, r, c] * keep
            copies.append(
                pltpu.make_async_copy(tiles.at[tile], out.at[:, cols], out_sems.at[tile])
            )
            copies[-1].start()
        for copy in copies:
            copy.wait()

    @pl.when(jnp.logical_not(general))
    def _():
        copy = pltpu.make_async_copy(a, out, out_sems.at[0])
        copy.start()
        copy.wait()


def shards(matrix, pivot_inv, pattern):
    f32, bf16 = jnp.float32, jnp.bfloat16
    in_hbm, in_vmem = pl.BlockSpec(memory_space=pltpu.HBM), pl.BlockSpec(memory_space=pltpu.VMEM)
    parts = pl.pallas_call(
        kernel,
        out_shape=[pltpu.VMEM(matrix.shape, f32)]
        + [pltpu.VMEM((1024, 512), bf16)] * 2
        + [pltpu.VMEM((512, 1024), bf16)] * 2,
        in_specs=[in_hbm] * 3,
        out_specs=[in_vmem] * 5,
        scratch_shapes=[
            pltpu.VMEM((TICKS_L, 4, 2, B // R, B), f32),
            pltpu.VMEM((64, 2, B // 2, B), f32),
            pltpu.VMEM(pivot_inv.shape, f32),
            pltpu.SMEM(pattern.shape, jnp.int32),
            pltpu.SemaphoreType.DMA((64 * R,)),
            pltpu.SemaphoreType.DMA((16 * R,)),
            pltpu.SemaphoreType.DMA((64 * R,)),
            pltpu.SemaphoreType.DMA((128,)),
            pltpu.SemaphoreType.DMA((4,)),
            pltpu.SemaphoreType.DMA((4,)),
            pltpu.SemaphoreType.DMA,
            pltpu.SemaphoreType.DMA((2,)),
            pltpu.SemaphoreType.DMA,
            pltpu.SemaphoreType.DMA((10,)),
        ],
        compiler_params=pltpu.CompilerParams(
            collective_id=0, has_side_effects=True, vmem_limit_bytes=50 << 20
        ),
        cost_estimate=pl.CostEstimate(
            flops=5 * 1024**3, bytes_accessed=8 << 20, transcendentals=0
        ),
        name="factor",
    )(matrix, pivot_inv, pattern)
    return pl.pallas_call(
        finish,
        out_shape=jax.ShapeDtypeStruct(matrix.shape, f32),
        in_specs=[in_vmem] * 5 + [in_hbm],
        out_specs=in_hbm,
        scratch_shapes=[
            pltpu.VMEM((4, 1024, 256), f32),
            pltpu.SMEM(pattern.shape, jnp.int32),
            pltpu.SemaphoreType.DMA,
            pltpu.SemaphoreType.DMA((4,)),
        ],
        compiler_params=pltpu.CompilerParams(vmem_limit_bytes=12 << 20),
        cost_estimate=pl.CostEstimate(
            flops=3 * 512 * 1024**2, bytes_accessed=8 << 20, transcendentals=0
        ),
        name="finish",
    )(*parts, pattern)


def solution(mesh):
    return jax.shard_map(
        shards,
        mesh=mesh,
        in_specs=(P("prow", "pcol"), P(), P("prow", "pcol")),
        out_specs=P("prow", "pcol"),
        check_vma=False,
    )
```

```python
import functools

import jax
import jax.numpy as jnp
from jax import lax
from jax.experimental import pallas as pl
from jax.experimental.pallas import tpu as pltpu
from jax.sharding import PartitionSpec as P

MESH = pl.DeviceIdType.MESH
B = 128
NX, NY, NZ = 4, 4, 8
R = 2
TICKS_L = 16 * R
LAG_U = 5

CHILD = (
    (105276967, 572662304, 201327138, 639633410),
    (1073746192, 1073844624, 29323537, 1073758436),
)
DEPTH = (
    (1515870810, 2995618556, 3456105856),
    (1515870810, 3219398634, 4294960132),
)
ROOT_WAY = (0, 2, 1, 3)


def bit(mask, n):
    low, high = mask & 0xFFFF, mask >> 16
    half = jnp.where(n >= 16, jnp.int32(high), jnp.int32(low))
    rest = lax.shift_right_logical(half, jnp.where(n >= 16, n - 16, n))
    return rest - 2 * lax.shift_right_logical(rest, 1)


def wrap(place, count):
    return jnp.where(place == count, 0, place)


def around(place, count):
    return wrap(place + 1, count), jnp.where(place == 0, count - 1, place - 1)


def lag(depth):
    return {2: 4, 4: 8}[R] * depth


def split(value):
    high = value.astype(jnp.bfloat16)
    return high, (value - high.astype(jnp.float32)).astype(jnp.bfloat16)


def dot3(a, b):
    (ah, al), (bh, bl) = a, b
    mul = functools.partial(jnp.dot, preferred_element_type=jnp.float32)
    return mul(ah, bl) + mul(al, bh) + mul(ah, bh)


def at(index, size=B):
    return pl.ds(pl.multiple_of(index * size, size), size)


def loop(count, body):
    def step(i, _):
        body(i)
        return 0

    lax.fori_loop(0, count, step, 0)


def kernel(
    a_hbm, pinv_hbm, pat_hbm, a, lhi, llo, uhi, ulo,
    lbuf, ubuf, pinv, pat,
    lrecv, crecv, hrecv, urecv, lsend, csend, hsend, usend, uhand, load_sems,
):
    p, q = lax.axis_index("prow"), lax.axis_index("pcol")
    y, z = lax.shift_right_logical(p, 1), lax.shift_right_logical(q, 2)
    core, x = p - 2 * y, q - NX * z
    is_root = (q == 0) | (p == 0)

    (xp, xm), (yp, ym), (zp, zm) = around(x, NX), around(y, NY), around(z, NZ)
    ways = (z * NX + xp, z * NX + xm, zp * NX + x, zm * NX + x)
    rows = (yp * 2 + core, ym * 2 + core)
    mate = y * 2 + 1 - core

    barrier = pltpu.get_barrier_semaphore()
    greet = [{"prow": mate, "pcol": q}] + [{"prow": r, "pcol": q} for r in rows]
    for w in ways:
        greet += [{"prow": p, "pcol": w}, {"prow": mate, "pcol": w}]
    for device in greet:
        pl.semaphore_signal(barrier, inc=1, device_id=device, device_id_type=MESH)

    load_pat = pltpu.make_async_copy(pat_hbm, pat, load_sems.at[8])
    load_pinv = pltpu.make_async_copy(pinv_hbm, pinv, load_sems.at[9])
    loads = [
        pltpu.make_async_copy(a_hbm.at[at(i)], a.at[at(i)], load_sems.at[i]) for i in range(8)
    ]
    load_pat.start()
    pl.when(is_root)(load_pinv.start)
    for load in loads:
        load.start()

    def part(index, count):
        return index if count is None else pl.ds(index, count)

    def copy_l(ref, send_sem, recv_sem, row, pcol):
        return pltpu.make_async_remote_copy(
            src_ref=ref,
            dst_ref=ref,
            send_sem=send_sem,
            recv_sem=recv_sem,
            device_id={"prow": row, "pcol": pcol},
            device_id_type=MESH,
        )

    def send_l(tick, t, way, both, count=None):
        ref = lbuf.at[part(tick, count), t]
        if not both:
            ref = lbuf.at[part(tick, count), t, 1]
        return copy_l(ref, lsend.at[way], lrecv.at[4 * tick + t], y * 2 + 1, ways[way])

    def send_leaf(even, tick, t, way):
        ref = lbuf.at[tick, t, 0]
        return copy_l(ref, lsend.at[way], hrecv.at[4 * even + t], y * 2, ways[way])

    def root_l(stream, tick, t, count=None):
        ref = lbuf.at[part(tick, count), t, stream]
        way = ROOT_WAY[t]
        return copy_l(ref, lsend.at[way], lrecv.at[4 * tick + t], y * 2 + 1, ways[way])

    def send_c(tick, t, way, count=None):
        ref = lbuf.at[part(tick, count), t, 0]
        return copy_l(ref, csend.at[way], crecv.at[4 * tick + t], y * 2 + 1, ways[way])

    def hand_l(tick, t, count=2):
        ref = lbuf.at[pl.ds(tick, count), t, 0]
        return copy_l(ref, hsend, hrecv.at[4 * tick + t], mate, q)

    def hand_ticks(tick, count):
        ref = lbuf.at[pl.ds(tick, count), :, 0]
        return copy_l(ref, hsend, hrecv.at[4 * tick], mate, q)

    def copy_u(ref, send_sem, slot, row):
        return pltpu.make_async_remote_copy(
            src_ref=ref,
            dst_ref=ref,
            send_sem=send_sem,
            recv_sem=urecv.at[slot],
            device_id={"prow": row, "pcol": q},
            device_id_type=MESH,
        )

    def send_u(slot, half, way):
        return copy_u(ubuf.at[slot, half], usend.at[way], 2 * slot + half, rows[way])

    def hand_u(slot, half):
        return copy_u(ubuf.at[slot, half], uhand, 2 * slot + half, mate)

    def end_u(sem, blocks):
        copy_u(ubuf.at[pl.ds(0, blocks)], sem, 0, mate).wait_send()

    def start_u(slot, ways_out):
        for half in (0, 1):
            for way in ways_out:
                send_u(slot, half, way).start()
            hand_u(slot, half).start()

    def wait_u(slot):
        for half in (0, 1):
            hand_u(slot, half).wait_recv()

    def put_u(slot, block):
        ubuf[slot] = block.reshape(2, B // 2, B)

    def get_u(slot):
        return ubuf[slot].reshape(B, B)

    def keep(i, j):
        return pat[i, j].astype(jnp.float32)

    def put_l(stream, block_tick, t, block):
        for h in range(R):
            rows_of = slice(h * (B // R), (h + 1) * (B // R))
            lbuf[block_tick * R + h, t, stream] = block[rows_of]

    def split_block(stream, block_tick, t, row, column):
        for h in range(R):
            hi, lo = split(lbuf[block_tick * R + h, t, stream])
            into = pl.ds(pl.multiple_of(row * B + h * (B // R), B // R), B // R)
            lhi[into, column * B : (column + 1) * B] = hi
            llo[into, column * B : (column + 1) * B] = lo

    childless = [(1 << 32) - 1 - functools.reduce(lambda m, n: m | n, CHILD[c]) for c in (0, 1)]

    used, tree_of, depth_of = [jnp.int32(0)] * 4, [jnp.int32(0)] * 4, [jnp.int32(0)] * 4
    first_of, leaf, to_leaf = [jnp.int32(0)] * 4, [jnp.int32(1)] * 4, [jnp.int32(0)] * 4
    mirrored = [
        wrap(NZ - zz, NZ) * NX + wrap(NX - xx, NX)
        for zz, xx in ((z, xp), (z, xm), (zp, x), (zm, x))
    ]
    depths = []
    for t in range(4):
        n = q if t < 2 else wrap(NZ - z, NZ) * NX + wrap(NX - x, NX)
        tree, flip = t % 2, 0 if t < 2 else 1
        depths.append(sum(bit(DEPTH[tree][b], n) * (1 << b) for b in range(3)))
        for w in range(4):
            has = bit(CHILD[tree][w ^ flip], n)
            first_of[w] = jnp.where((has == 1) & (leaf[t] == 1), 1, first_of[w])
            leaf[t] = jnp.where(has == 1, 0, leaf[t])
            used[w] = used[w] + has
            tree_of[w] = tree_of[w] + has * t
            depth_of[w] = depth_of[w] + has * depths[t]
            to = ways[w] if t < 2 else mirrored[w]
            to_leaf[w] = to_leaf[w] + has * bit(childless[tree], to)
    deepest = jnp.maximum(functools.reduce(jnp.maximum, depths), 5)

    def right(pair, stream):
        if stream == 1:
            loop(16, lambda i: wait_u(pair * 16 + i))

        def split_right(i):
            for h in (0, 1):
                for half in (0, 1):
                    j = 4 * half + i
                    hi, lo = split(get_u((2 * pair + h) * 8 + j))
                    uhi[h * B : (h + 1) * B, at(j)] = hi
                    ulo[h * B : (h + 1) * B, at(j)] = lo

        loop(4, split_right)

    def split_left(pair, half, stream):
        def body(i):
            for h in (0, 1):
                split_block(stream, 4 * pair + 2 * h + half, i, 4 * half + i, h)

        loop(4, body)

    def piece(n, halves, stream):
        pair = lax.shift_right_logical(n, 2)
        tile = n - 4 * pair

        @pl.when(tile == 0)
        def _():
            if 0 in halves:
                pl.when(pair < 3)(lambda: right(pair, stream))
            if stream == 0:

                def wait_tick(i):
                    for t in range(4):
                        hand_l(pair * 4 * R + 2 * i, t).wait_recv()

                loop(2 * R, wait_tick)
            for half in halves:
                split_left(pair, half, stream)

        @pl.when(pair < 3)
        def _():
            r, cols = slice(halves[0] * 512, (halves[-1] + 1) * 512), at(tile, 256)
            a[r, cols] -= dot3(
                (lhi[r, 0:256], llo[r, 0:256]), (uhi[0:256, cols], ulo[0:256, cols])
            )

        if 1 in halves:
            pl.when((pair == 2) & (tile == 3))(lambda: right(3, stream))

    def general0():
        first = 2 * deepest + 2

        def relay(tick, way):
            row = lax.shift_right_logical(tick, 2)
            slot = 4 * row + 4 * way + tick
            for half in (0, 1):
                hand_u(slot, half).wait_recv()
                on = y < NY - 1 if way == 0 else y > 1
                pl.when(on)(lambda: send_u(slot, half, way).start())
                hand_u(slot, half).start()

        def step(kk):
            for odd in (0, 1):
                for way in (0, 1):
                    tick = 2 * kk + odd - LAG_U * (y if way == 0 else NY - y)
                    pl.when((tick >= 0) & (tick < 32))(lambda: relay(tick, way))
            pl.when(kk >= first)(lambda: piece(kk - first, (0, 1), 0))

        loop(first + 13, step)
        pl.when(y < NY - 1)(lambda: end_u(usend.at[0], 32))
        pl.when(y > 1)(lambda: end_u(usend.at[1], 32))
        end_u(uhand, 64)

    def general1(both):
        start = lag(deepest) + 4 * R + (0 if both else 4 * R)
        first_piece = lax.shift_right_logical(start, 1)
        ticks = TICKS_L + (0 if both else 4 * R)

        def receive(i, t, odd, is_leaf):
            def hand():
                if odd:
                    hand_l(i - 1, t).start()

            if both:
                send_l(i, t, 0, not is_leaf).wait_recv()
                if not is_leaf:
                    hand()
                return

            @pl.when(i < 4 * R)
            def _():
                send_c(i, t, 0).wait_recv()
                hand()

            pl.when(i >= 4 * R)(lambda: send_l(i - 4 * R, t, 0, False).wait_recv())

        def forward(i, way, odd):
            t = tree_of[way]
            if both:
                pl.when(to_leaf[way] == 0)(lambda: send_l(i, t, way, True).start())

                @pl.when(to_leaf[way] == 1)
                def _():
                    send_leaf(i - 1 if odd else i, i, t, way).start()
                    send_l(i, t, way, False).start()

                return
            pl.when(i < 4 * R)(lambda: send_c(i, t, way).start())
            pl.when(i >= 4 * R)(lambda: send_l(i - 4 * R, t, way, False).start())

        last = [jnp.where(used[way] == 1, ticks, 0) for way in range(4)]
        last_leaf = [jnp.where(leaf[t] == 1, ticks, 0) for t in range(4)]
        lags = [lag(d) for d in depths]
        lags_out = [lag(d) for d in depth_of]

        def relay(k, odd):
            for way in range(4):
                i = k - lags_out[way]

                @pl.when((i >= 0) & (i < last[way]))
                def _():
                    pl.when(first_of[way] == 1)(lambda: receive(i, tree_of[way], odd, False))
                    forward(i, way, odd)

            for t in range(4):
                i = k - lags[t]
                pl.when((i >= 0) & (i < last_leaf[t]))(lambda: receive(i, t, odd, True))

        def step(kk):
            for odd in (0, 1):
                relay(2 * kk + odd, odd == 1)
                pl.when(kk >= first_piece)(lambda: piece(kk - first_piece, (odd,), 1))

        loop(first_piece + 13, step)
        for way in range(4):

            @pl.when(used[way] == 1)
            def _():
                send_l(0, 0, way, both, TICKS_L).wait_send()
                if not both:
                    send_c(0, 0, way, 4 * R).wait_send()

        if both:
            handed = 4 - sum(leaf)
            for count in range(1, 5):
                pl.when(handed == count)(
                    lambda: copy_l(lbuf.at[:, pl.ds(0, count), 0], hsend, hrecv.at[0], mate, q).wait_send()
                )
        else:
            hand_ticks(0, 4 * R).wait_send()

    def mask_block(i, j):
        block = a[at(i), at(j)] * keep(i, j)
        a[at(i), at(j)] = block
        return block

    def send_row(kb):
        for j in range(4):
            for half in (0, 1):
                for way in (0, 1):
                    slot = kb * 8 + 4 * way + j
                    send_u(slot, half, way).start()
                    hand_u(slot, half).start()

    def prepare_upper():
        def body(j):
            for kb in range(4):
                put_u(kb * 8 + j, mask_block(kb, j))

        loop(8, body)

    def upper_root():
        loop(4, send_row)
        for kb in range(4):
            r = slice(kb * B, (kb + 1) * B)
            uhi[r, :], ulo[r, :] = split(dot3(split(pinv[kb]), split(a[r, :])))

        def second(i):
            for t in range(4):
                for h in range(0, R, 2):
                    hand_l(i * R + h, t).wait_recv()
                split_block(0, i, t, 0, t)
            prod = dot3((lhi[0:B, :], llo[0:B, :]), (uhi[...], ulo[...]))
            for j in range(8):
                c = slice(j * B, (j + 1) * B)
                block = (a[at(4 + i), c] - prod[:, c]) * keep(4 + i, j)
                a[at(4 + i), c] = block
                put_u((4 + i) * 8 + j, block)
            send_row(4 + i)

        loop(4, second)
        for way in (0, 1):
            end_u(usend.at[way], 32)
        end_u(uhand, 64)

    def prepare_corner():
        def body(i):
            for t in range(4):
                put_l(0, i, t, mask_block(4 + i, t))
                put_u(t * 8 + 4 + i, mask_block(t, 4 + i))

        loop(4, body)

    def corner():
        def start(i):
            for h in range(R):
                for t in range(4):
                    send_c(i * R + h, t, ROOT_WAY[t]).start()
            for kb in range(4):
                for half in (0, 1):
                    for way in (0, 1):
                        send_u(kb * 8 + 4 + i, half, way).start()

        loop(4, start)
        for way in range(4):
            send_c(0, 0, way, 4 * R).wait_send()

        def hand(i):
            for kb in range(4):
                for half in (0, 1):
                    hand_u(kb * 8 + 4 + i, half).start()

        loop(4, hand)

        def rest(i):
            for j in range(4):
                mask_block(i, j)

        loop(4, rest)
        for kb in range(4):
            c = slice(kb * B, (kb + 1) * B)
            low = dot3(split(a[512:1024, c]), split(pinv[kb]))
            a[512:1024, c] = low
            lhi[512:1024, c], llo[512:1024, c] = split(low)
        for j in range(4):
            c = slice((4 + j) * B, (5 + j) * B)
            prod = dot3((lhi[512:1024, :], llo[512:1024, :]), split(a[0:512, c]))
            for i in range(4):
                r = slice((4 + i) * B, (5 + i) * B)
                a[r, c] = (a[r, c] - prod[i * B : (i + 1) * B]) * keep(4 + i, 4 + j)
        for way in (0, 1):
            end_u(usend.at[way], 16)
        end_u(uhand, 16)

    def put_column(stream, kb, low):
        a[:, at(kb)] = low
        for i in range(8):
            put_l(stream, 2 * kb + i // 4, i % 4, low[i * B : (i + 1) * B])

    def lower_first(stream, kb):
        loop(8, lambda i: mask_block(i, kb))
        put_column(stream, kb, dot3(split(a[:, at(kb)]), split(pinv[kb])))

    def lower_root(stream, both):
        def send_column(kb):
            for i in range(2 * R):
                for t in range(4):
                    root_l(stream, kb * 2 * R + i, t).start()

        if not both:
            for kb in range(4):
                wait_u(kb * 8 + 4)
        send_column(0)

        def first(kb):
            lower_first(stream, kb + 1)
            send_column(kb + 1)

        loop(3, first)
        lhi[...], llo[...] = split(a[:, 0:512])

        def second(j):
            def arrive():
                for kb in range(4):
                    slot = kb * 8 + 4 + j
                    for half in (0, 1):
                        hand_u(slot, half).wait_recv()
                        if stream == 0:
                            pl.when((y == 1) if kb < 2 else (y == 3))(
                                lambda: send_u(slot, half, 0 if kb < 2 else 1).start()
                            )
                            hand_u(slot, half).start()

            if both:
                arrive()
            else:
                pl.when(j > 0)(arrive)
            for kb in range(4):
                r = slice(kb * B, (kb + 1) * B)
                uhi[r, 0:B], ulo[r, 0:B] = split(get_u(kb * 8 + 4 + j))
            c = at(4 + j)
            prod = dot3((lhi[...], llo[...]), (uhi[:, 0:B], ulo[:, 0:B]))
            for i in range(8):
                r = slice(i * B, (i + 1) * B)
                a[r, c] = (a[r, c] - prod[r]) * keep(i, 4 + j)
            put_column(stream, 4 + j, dot3(split(a[:, c]), split(pinv[4 + j])))
            send_column(4 + j)

        loop(4, second)
        if stream == 0:
            end_u(uhand, 16)
            pl.when(y == 1)(lambda: end_u(usend.at[0], 8))
            pl.when(y == 3)(lambda: end_u(usend.at[1], 8))
        for t in range(4):
            root_l(stream, 0, t, TICKS_L).wait_send()

    is_corner, is_upper = (q == 0) & (p == 0), (q > 0) & (p == 0)
    lower0, lower1 = (q == 0) & (core == 0) & (p > 0), (q == 0) & (core == 1)
    for load in loads:
        load.wait()
    load_pat.wait()
    pl.when(is_root)(load_pinv.wait)
    pl.when(is_corner)(prepare_corner)
    pl.when(is_upper)(prepare_upper)
    pl.when(lower0)(lambda: lower_first(0, 0))
    pl.when(lower1)(lambda: lower_first(1, 0))
    pl.semaphore_wait(barrier, len(greet))

    pl.when(is_corner)(corner)
    pl.when(is_upper)(upper_root)
    pl.when(lower0)(lambda: lower_root(0, True))
    pl.when(lower1 & (p == 1))(lambda: lower_root(1, False))
    pl.when(lower1 & (p > 1))(lambda: lower_root(1, True))
    pl.when((q > 0) & (core == 0) & (p > 0))(general0)
    pl.when((q > 0) & (p == 1))(lambda: general1(False))
    pl.when((q > 0) & (core == 1) & (p > 1))(lambda: general1(True))


def finish(a, lhi, llo, uhi, ulo, pat_hbm, out, tiles, pat, pat_sem, out_sems):
    general = (lax.axis_index("prow") > 0) & (lax.axis_index("pcol") > 0)

    @pl.when(general)
    def _():
        load = pltpu.make_async_copy(pat_hbm, pat, pat_sem)
        load.start()
        copies = []
        for tile in range(4):
            cols = slice(tile * 256, (tile + 1) * 256)
            right = (uhi[0:256, cols], ulo[0:256, cols])
            tiles[tile] = a[:, cols] - dot3((lhi[:, 0:256], llo[:, 0:256]), right)
            if tile == 0:
                load.wait()
            for i in range(8):
                for h in (0, 1):
                    r, c = slice(i * B, (i + 1) * B), slice(h * B, (h + 1) * B)
                    keep = pat[i, 2 * tile + h].astype(jnp.float32)
                    tiles[tile, r, c] = tiles[tile, r, c] * keep
            copies.append(
                pltpu.make_async_copy(tiles.at[tile], out.at[:, cols], out_sems.at[tile])
            )
            copies[-1].start()
        for copy in copies:
            copy.wait()

    @pl.when(jnp.logical_not(general))
    def _():
        copy = pltpu.make_async_copy(a, out, out_sems.at[0])
        copy.start()
        copy.wait()


def shards(matrix, pivot_inv, pattern):
    f32, bf16 = jnp.float32, jnp.bfloat16
    in_hbm, in_vmem = pl.BlockSpec(memory_space=pltpu.HBM), pl.BlockSpec(memory_space=pltpu.VMEM)
    parts = pl.pallas_call(
        kernel,
        out_shape=[pltpu.VMEM(matrix.shape, f32)]
        + [pltpu.VMEM((1024, 512), bf16)] * 2
        + [pltpu.VMEM((512, 1024), bf16)] * 2,
        in_specs=[in_hbm] * 3,
        out_specs=[in_vmem] * 5,
        scratch_shapes=[
            pltpu.VMEM((TICKS_L, 4, 2, B // R, B), f32),
            pltpu.VMEM((64, 2, B // 2, B), f32),
            pltpu.VMEM(pivot_inv.shape, f32),
            pltpu.SMEM(pattern.shape, jnp.int32),
            pltpu.SemaphoreType.DMA((64 * R,)),
            pltpu.SemaphoreType.DMA((16 * R,)),
            pltpu.SemaphoreType.DMA((64 * R,)),
            pltpu.SemaphoreType.DMA((128,)),
            pltpu.SemaphoreType.DMA((4,)),
            pltpu.SemaphoreType.DMA((4,)),
            pltpu.SemaphoreType.DMA,
            pltpu.SemaphoreType.DMA((2,)),
            pltpu.SemaphoreType.DMA,
            pltpu.SemaphoreType.DMA((10,)),
        ],
        compiler_params=pltpu.CompilerParams(
            collective_id=0, has_side_effects=True, vmem_limit_bytes=50 << 20
        ),
        cost_estimate=pl.CostEstimate(
            flops=5 * 1024**3, bytes_accessed=8 << 20, transcendentals=0
        ),
        name="factor",
    )(matrix, pivot_inv, pattern)
    return pl.pallas_call(
        finish,
        out_shape=jax.ShapeDtypeStruct(matrix.shape, f32),
        in_specs=[in_vmem] * 5 + [in_hbm],
        out_specs=in_hbm,
        scratch_shapes=[
            pltpu.VMEM((4, 1024, 256), f32),
            pltpu.SMEM(pattern.shape, jnp.int32),
            pltpu.SemaphoreType.DMA,
            pltpu.SemaphoreType.DMA((4,)),
        ],
        compiler_params=pltpu.CompilerParams(vmem_limit_bytes=12 << 20),
        cost_estimate=pl.CostEstimate(
            flops=3 * 512 * 1024**2, bytes_accessed=8 << 20, transcendentals=0
        ),
        name="finish",
    )(*parts, pattern)


def solution(mesh):
    return jax.shard_map(
        shards,
        mesh=mesh,
        in_specs=(P("prow", "pcol"), P(), P("prow", "pcol")),
        out_specs=P("prow", "pcol"),
        check_vma=False,
    )
```

```python
import functools

import jax
import jax.numpy as jnp
from jax import lax
from jax.experimental import pallas as pl
from jax.experimental.pallas import tpu as pltpu
from jax.sharding import PartitionSpec as P

MESH = pl.DeviceIdType.MESH
B = 128
NX, NY, NZ = 4, 4, 8
R = 2
TICKS_L = 16 * R
LAG_U = 5

CHILD = (
    (105276967, 572662304, 201327138, 639633410),
    (1073746192, 1073844624, 29323537, 1073758436),
)
DEPTH = (
    (1515870810, 2995618556, 3456105856),
    (1515870810, 3219398634, 4294960132),
)
ROOT_WAY = (0, 2, 1, 3)


def bit(mask, n):
    low, high = mask & 0xFFFF, mask >> 16
    half = jnp.where(n >= 16, jnp.int32(high), jnp.int32(low))
    rest = lax.shift_right_logical(half, jnp.where(n >= 16, n - 16, n))
    return rest - 2 * lax.shift_right_logical(rest, 1)


def wrap(place, count):
    return jnp.where(place == count, 0, place)


def around(place, count):
    return wrap(place + 1, count), jnp.where(place == 0, count - 1, place - 1)


def lag(depth):
    return {2: 4, 4: 8}[R] * depth


def split(value):
    high = value.astype(jnp.bfloat16)
    return high, (value - high.astype(jnp.float32)).astype(jnp.bfloat16)


def dot3(a, b):
    (ah, al), (bh, bl) = a, b
    mul = functools.partial(jnp.dot, preferred_element_type=jnp.float32)
    return mul(ah, bl) + mul(al, bh) + mul(ah, bh)


def at(index, size=B):
    return pl.ds(pl.multiple_of(index * size, size), size)


def loop(count, body):
    def step(i, _):
        body(i)
        return 0

    lax.fori_loop(0, count, step, 0)


def kernel(
    a_hbm, pinv_hbm, pat_hbm, a, lhi, llo, uhi, ulo,
    lbuf, ubuf, pinv, pat,
    lrecv, crecv, hrecv, urecv, lsend, csend, hsend, usend, uhand, load_sems,
):
    p, q = lax.axis_index("prow"), lax.axis_index("pcol")
    y, z = lax.shift_right_logical(p, 1), lax.shift_right_logical(q, 2)
    core, x = p - 2 * y, q - NX * z
    is_root = (q == 0) | (p == 0)

    (xp, xm), (yp, ym), (zp, zm) = around(x, NX), around(y, NY), around(z, NZ)
    ways = (z * NX + xp, z * NX + xm, zp * NX + x, zm * NX + x)
    rows = (yp * 2 + core, ym * 2 + core)
    mate = y * 2 + 1 - core

    barrier = pltpu.get_barrier_semaphore()
    greet = [{"prow": mate, "pcol": q}] + [{"prow": r, "pcol": q} for r in rows]
    for w in ways:
        greet += [{"prow": p, "pcol": w}, {"prow": mate, "pcol": w}]
    for device in greet:
        pl.semaphore_signal(barrier, inc=1, device_id=device, device_id_type=MESH)

    load_pat = pltpu.make_async_copy(pat_hbm, pat, load_sems.at[8])
    load_pinv = pltpu.make_async_copy(pinv_hbm, pinv, load_sems.at[9])
    loads = [
        pltpu.make_async_copy(a_hbm.at[at(i)], a.at[at(i)], load_sems.at[i]) for i in range(8)
    ]
    load_pat.start()
    pl.when(is_root)(load_pinv.start)
    for load in loads:
        load.start()

    def part(index, count):
        return index if count is None else pl.ds(index, count)

    def copy_l(ref, send_sem, recv_sem, row, pcol):
        return pltpu.make_async_remote_copy(
            src_ref=ref,
            dst_ref=ref,
            send_sem=send_sem,
            recv_sem=recv_sem,
            device_id={"prow": row, "pcol": pcol},
            device_id_type=MESH,
        )

    def send_l(tick, t, way, both, count=None):
        ref = lbuf.at[part(tick, count), t]
        if not both:
            ref = lbuf.at[part(tick, count), t, 1]
        return copy_l(ref, lsend.at[way], lrecv.at[4 * tick + t], y * 2 + 1, ways[way])

    def send_leaf(even, tick, t, way):
        ref = lbuf.at[tick, t, 0]
        return copy_l(ref, lsend.at[way], hrecv.at[4 * even + t], y * 2, ways[way])

    def root_l(stream, tick, t, count=None):
        ref = lbuf.at[part(tick, count), t, stream]
        way = ROOT_WAY[t]
        return copy_l(ref, lsend.at[way], lrecv.at[4 * tick + t], y * 2 + 1, ways[way])

    def send_c(tick, t, way, count=None):
        ref = lbuf.at[part(tick, count), t, 0]
        return copy_l(ref, csend.at[way], crecv.at[4 * tick + t], y * 2 + 1, ways[way])

    def hand_l(tick, t, count=2):
        ref = lbuf.at[pl.ds(tick, count), t, 0]
        return copy_l(ref, hsend, hrecv.at[4 * tick + t], mate, q)

    def hand_ticks(tick, count):
        ref = lbuf.at[pl.ds(tick, count), :, 0]
        return copy_l(ref, hsend, hrecv.at[4 * tick], mate, q)

    def copy_u(ref, send_sem, slot, row):
        return pltpu.make_async_remote_copy(
            src_ref=ref,
            dst_ref=ref,
            send_sem=send_sem,
            recv_sem=urecv.at[slot],
            device_id={"prow": row, "pcol": q},
            device_id_type=MESH,
        )

    def send_u(slot, half, way):
        return copy_u(ubuf.at[slot, half], usend.at[way], 2 * slot + half, rows[way])

    def hand_u(slot, half):
        return copy_u(ubuf.at[slot, half], uhand, 2 * slot + half, mate)

    def end_u(sem, blocks):
        copy_u(ubuf.at[pl.ds(0, blocks)], sem, 0, mate).wait_send()

    def start_u(slot, ways_out):
        for half in (0, 1):
            for way in ways_out:
                send_u(slot, half, way).start()
            hand_u(slot, half).start()

    def wait_u(slot):
        for half in (0, 1):
            hand_u(slot, half).wait_recv()

    def put_u(slot, block):
        ubuf[slot] = block.reshape(2, B // 2, B)

    def get_u(slot):
        return ubuf[slot].reshape(B, B)

    def keep(i, j):
        return pat[i, j].astype(jnp.float32)

    def put_l(stream, block_tick, t, block):
        for h in range(R):
            rows_of = slice(h * (B // R), (h + 1) * (B // R))
            lbuf[block_tick * R + h, t, stream] = block[rows_of]

    def split_block(stream, block_tick, t, row, column):
        for h in range(R):
            hi, lo = split(lbuf[block_tick * R + h, t, stream])
            into = pl.ds(pl.multiple_of(row * B + h * (B // R), B // R), B // R)
            lhi[into, column * B : (column + 1) * B] = hi
            llo[into, column * B : (column + 1) * B] = lo

    childless = [(1 << 32) - 1 - functools.reduce(lambda m, n: m | n, CHILD[c]) for c in (0, 1)]

    used, tree_of, depth_of = [jnp.int32(0)] * 4, [jnp.int32(0)] * 4, [jnp.int32(0)] * 4
    first_of, leaf, to_leaf = [jnp.int32(0)] * 4, [jnp.int32(1)] * 4, [jnp.int32(0)] * 4
    mirrored = [
        wrap(NZ - zz, NZ) * NX + wrap(NX - xx, NX)
        for zz, xx in ((z, xp), (z, xm), (zp, x), (zm, x))
    ]
    depths = []
    for t in range(4):
        n = q if t < 2 else wrap(NZ - z, NZ) * NX + wrap(NX - x, NX)
        tree, flip = t % 2, 0 if t < 2 else 1
        depths.append(sum(bit(DEPTH[tree][b], n) * (1 << b) for b in range(3)))
        for w in range(4):
            has = bit(CHILD[tree][w ^ flip], n)
            first_of[w] = jnp.where((has == 1) & (leaf[t] == 1), 1, first_of[w])
            leaf[t] = jnp.where(has == 1, 0, leaf[t])
            used[w] = used[w] + has
            tree_of[w] = tree_of[w] + has * t
            depth_of[w] = depth_of[w] + has * depths[t]
            to = ways[w] if t < 2 else mirrored[w]
            to_leaf[w] = to_leaf[w] + has * bit(childless[tree], to)
    deepest = jnp.maximum(functools.reduce(jnp.maximum, depths), 5)

    def right(pair, stream):
        if stream == 1:
            loop(16, lambda i: wait_u(pair * 16 + i))

        def split_right(i):
            for h in (0, 1):
                for half in (0, 1):
                    j = 4 * half + i
                    hi, lo = split(get_u((2 * pair + h) * 8 + j))
                    uhi[h * B : (h + 1) * B, at(j)] = hi
                    ulo[h * B : (h + 1) * B, at(j)] = lo

        loop(4, split_right)

    def split_left(pair, half, stream):
        def body(i):
            for h in (0, 1):
                split_block(stream, 4 * pair + 2 * h + half, i, 4 * half + i, h)

        loop(4, body)

    def piece(n, halves, stream):
        pair = lax.shift_right_logical(n, 2)
        tile = n - 4 * pair

        @pl.when(tile == 0)
        def _():
            if 0 in halves:
                pl.when(pair < 3)(lambda: right(pair, stream))
            if stream == 0:

                def wait_tick(i):
                    for t in range(4):
                        hand_l(pair * 4 * R + 2 * i, t).wait_recv()

                loop(2 * R, wait_tick)
            for half in halves:
                split_left(pair, half, stream)

        @pl.when(pair < 3)
        def _():
            r, cols = slice(halves[0] * 512, (halves[-1] + 1) * 512), at(tile, 256)
            a[r, cols] -= dot3(
                (lhi[r, 0:256], llo[r, 0:256]), (uhi[0:256, cols], ulo[0:256, cols])
            )

        if 1 in halves:
            pl.when((pair == 2) & (tile == 3))(lambda: right(3, stream))

    def general0():
        first = 2 * deepest + 2

        def relay(tick, way):
            row = lax.shift_right_logical(tick, 2)
            slot = 4 * row + 4 * way + tick
            for half in (0, 1):
                hand_u(slot, half).wait_recv()
                on = y < NY - 1 if way == 0 else y > 1
                pl.when(on)(lambda: send_u(slot, half, way).start())
                hand_u(slot, half).start()

        def step(kk):
            for odd in (0, 1):
                for way in (0, 1):
                    tick = 2 * kk + odd - LAG_U * (y if way == 0 else NY - y)
                    pl.when((tick >= 0) & (tick < 32))(lambda: relay(tick, way))
            pl.when(kk >= first)(lambda: piece(kk - first, (0, 1), 0))

        loop(first + 13, step)
        pl.when(y < NY - 1)(lambda: end_u(usend.at[0], 32))
        pl.when(y > 1)(lambda: end_u(usend.at[1], 32))
        end_u(uhand, 64)

    def general1(both):
        start = lag(deepest) + 4 * R + (0 if both else 4 * R)
        first_piece = lax.shift_right_logical(start, 1)
        ticks = TICKS_L + (0 if both else 4 * R)

        def receive(i, t, odd, is_leaf):
            def hand():
                if odd:
                    hand_l(i - 1, t).start()

            if both:
                send_l(i, t, 0, not is_leaf).wait_recv()
                if not is_leaf:
                    hand()
                return

            @pl.when(i < 4 * R)
            def _():
                send_c(i, t, 0).wait_recv()
                hand()

            pl.when(i >= 4 * R)(lambda: send_l(i - 4 * R, t, 0, False).wait_recv())

        def forward(i, way, odd):
            t = tree_of[way]
            if both:
                pl.when(to_leaf[way] == 0)(lambda: send_l(i, t, way, True).start())

                @pl.when(to_leaf[way] == 1)
                def _():
                    send_leaf(i - 1 if odd else i, i, t, way).start()
                    send_l(i, t, way, False).start()

                return
            pl.when(i < 4 * R)(lambda: send_c(i, t, way).start())
            pl.when(i >= 4 * R)(lambda: send_l(i - 4 * R, t, way, False).start())

        last = [jnp.where(used[way] == 1, ticks, 0) for way in range(4)]
        last_leaf = [jnp.where(leaf[t] == 1, ticks, 0) for t in range(4)]
        lags = [lag(d) for d in depths]
        lags_out = [lag(d) for d in depth_of]

        def relay(k, odd):
            for way in range(4):
                i = k - lags_out[way]

                @pl.when((i >= 0) & (i < last[way]))
                def _():
                    pl.when(first_of[way] == 1)(lambda: receive(i, tree_of[way], odd, False))
                    forward(i, way, odd)

            for t in range(4):
                i = k - lags[t]
                pl.when((i >= 0) & (i < last_leaf[t]))(lambda: receive(i, t, odd, True))

        def step(kk):
            for odd in (0, 1):
                relay(2 * kk + odd, odd == 1)
                pl.when(kk >= first_piece)(lambda: piece(kk - first_piece, (odd,), 1))

        loop(first_piece + 13, step)
        for way in range(4):

            @pl.when(used[way] == 1)
            def _():
                send_l(0, 0, way, both, TICKS_L).wait_send()
                if not both:
                    send_c(0, 0, way, 4 * R).wait_send()

        if both:
            handed = 4 - sum(leaf)
            for count in range(1, 5):
                pl.when(handed == count)(
                    lambda: copy_l(lbuf.at[:, pl.ds(0, count), 0], hsend, hrecv.at[0], mate, q).wait_send()
                )
        else:
            hand_ticks(0, 4 * R).wait_send()

    def mask_block(i, j):
        block = a[at(i), at(j)] * keep(i, j)
        a[at(i), at(j)] = block
        return block

    def send_row(kb):
        for j in range(4):
            for half in (0, 1):
                for way in (0, 1):
                    slot = kb * 8 + 4 * way + j
                    send_u(slot, half, way).start()
                    hand_u(slot, half).start()

    def prepare_upper():
        def body(j):
            for kb in range(4):
                put_u(kb * 8 + j, mask_block(kb, j))

        loop(8, body)

    def upper_root():
        loop(4, send_row)
        for kb in range(4):
            r = slice(kb * B, (kb + 1) * B)
            uhi[r, :], ulo[r, :] = split(dot3(split(pinv[kb]), split(a[r, :])))

        def second(i):
            for t in range(4):
                for h in range(0, R, 2):
                    hand_l(i * R + h, t).wait_recv()
                split_block(0, i, t, 0, t)
            prod = dot3((lhi[0:B, :], llo[0:B, :]), (uhi[...], ulo[...]))
            for j in range(8):
                c = slice(j * B, (j + 1) * B)
                block = (a[at(4 + i), c] - prod[:, c]) * keep(4 + i, j)
                a[at(4 + i), c] = block
                put_u((4 + i) * 8 + j, block)
            send_row(4 + i)

        loop(4, second)
        for way in (0, 1):
            end_u(usend.at[way], 32)
        end_u(uhand, 64)

    def prepare_corner():
        def body(i):
            for t in range(4):
                put_l(0, i, t, mask_block(4 + i, t))
                put_u(t * 8 + 4 + i, mask_block(t, 4 + i))

        loop(4, body)

    def corner():
        def start(i):
            for h in range(R):
                for t in range(4):
                    send_c(i * R + h, t, ROOT_WAY[t]).start()
            for kb in range(4):
                for half in (0, 1):
                    for way in (0, 1):
                        send_u(kb * 8 + 4 + i, half, way).start()

        loop(4, start)
        for way in range(4):
            send_c(0, 0, way, 4 * R).wait_send()

        def hand(i):
            for kb in range(4):
                for half in (0, 1):
                    hand_u(kb * 8 + 4 + i, half).start()

        loop(4, hand)

        def rest(i):
            for j in range(4):
                mask_block(i, j)

        loop(4, rest)
        for kb in range(4):
            c = slice(kb * B, (kb + 1) * B)
            low = dot3(split(a[512:1024, c]), split(pinv[kb]))
            a[512:1024, c] = low
            lhi[512:1024, c], llo[512:1024, c] = split(low)
        for j in range(4):
            c = slice((4 + j) * B, (5 + j) * B)
            prod = dot3((lhi[512:1024, :], llo[512:1024, :]), split(a[0:512, c]))
            for i in range(4):
                r = slice((4 + i) * B, (5 + i) * B)
                a[r, c] = (a[r, c] - prod[i * B : (i + 1) * B]) * keep(4 + i, 4 + j)
        for way in (0, 1):
            end_u(usend.at[way], 16)
        end_u(uhand, 16)

    def put_column(stream, kb, low):
        a[:, at(kb)] = low
        for i in range(8):
            put_l(stream, 2 * kb + i // 4, i % 4, low[i * B : (i + 1) * B])

    def lower_first(stream, kb):
        loop(8, lambda i: mask_block(i, kb))
        put_column(stream, kb, dot3(split(a[:, at(kb)]), split(pinv[kb])))

    def lower_root(stream, both):
        def send_column(kb):
            for i in range(2 * R):
                for t in range(4):
                    root_l(stream, kb * 2 * R + i, t).start()

        if not both:
            for kb in range(4):
                wait_u(kb * 8 + 4)
        send_column(0)

        def first(kb):
            lower_first(stream, kb + 1)
            send_column(kb + 1)

        loop(3, first)
        lhi[...], llo[...] = split(a[:, 0:512])

        def second(j):
            def arrive():
                for kb in range(4):
                    slot = kb * 8 + 4 + j
                    for half in (0, 1):
                        hand_u(slot, half).wait_recv()
                        if stream == 0:
                            pl.when((y == 1) if kb < 2 else (y == 3))(
                                lambda: send_u(slot, half, 0 if kb < 2 else 1).start()
                            )
                            hand_u(slot, half).start()

            if both:
                arrive()
            else:
                pl.when(j > 0)(arrive)
            for kb in range(4):
                r = slice(kb * B, (kb + 1) * B)
                uhi[r, 0:B], ulo[r, 0:B] = split(get_u(kb * 8 + 4 + j))
            c = at(4 + j)
            prod = dot3((lhi[...], llo[...]), (uhi[:, 0:B], ulo[:, 0:B]))
            for i in range(8):
                r = slice(i * B, (i + 1) * B)
                a[r, c] = (a[r, c] - prod[r]) * keep(i, 4 + j)
            put_column(stream, 4 + j, dot3(split(a[:, c]), split(pinv[4 + j])))
            send_column(4 + j)

        loop(4, second)
        if stream == 0:
            end_u(uhand, 16)
            pl.when(y == 1)(lambda: end_u(usend.at[0], 8))
            pl.when(y == 3)(lambda: end_u(usend.at[1], 8))
        for t in range(4):
            root_l(stream, 0, t, TICKS_L).wait_send()

    is_corner, is_upper = (q == 0) & (p == 0), (q > 0) & (p == 0)
    lower0, lower1 = (q == 0) & (core == 0) & (p > 0), (q == 0) & (core == 1)
    for load in loads:
        load.wait()
    load_pat.wait()
    pl.when(is_root)(load_pinv.wait)
    pl.when(is_corner)(prepare_corner)
    pl.when(is_upper)(prepare_upper)
    pl.when(lower0)(lambda: lower_first(0, 0))
    pl.when(lower1)(lambda: lower_first(1, 0))
    pl.semaphore_wait(barrier, len(greet))

    pl.when(is_corner)(corner)
    pl.when(is_upper)(upper_root)
    pl.when(lower0)(lambda: lower_root(0, True))
    pl.when(lower1 & (p == 1))(lambda: lower_root(1, False))
    pl.when(lower1 & (p > 1))(lambda: lower_root(1, True))
    pl.when((q > 0) & (core == 0) & (p > 0))(general0)
    pl.when((q > 0) & (p == 1))(lambda: general1(False))
    pl.when((q > 0) & (core == 1) & (p > 1))(lambda: general1(True))


def finish(a, lhi, llo, uhi, ulo, pat_hbm, out, tiles, pat, pat_sem, out_sems):
    general = (lax.axis_index("prow") > 0) & (lax.axis_index("pcol") > 0)

    @pl.when(general)
    def _():
        load = pltpu.make_async_copy(pat_hbm, pat, pat_sem)
        load.start()
        copies = []
        for n, (first, last) in enumerate(((0, 512), (512, 768), (768, 1024))):
            cols = slice(first, last)
            right = (uhi[0:256, cols], ulo[0:256, cols])
            tiles[:, cols] = a[:, cols] - dot3((lhi[:, 0:256], llo[:, 0:256]), right)
            if n == 0:
                load.wait()
            for i in range(8):
                for j in range(first // B, last // B):
                    r, c = slice(i * B, (i + 1) * B), slice(j * B, (j + 1) * B)
                    tiles[r, c] = tiles[r, c] * pat[i, j].astype(jnp.float32)
            copies.append(
                pltpu.make_async_copy(tiles.at[:, cols], out.at[:, cols], out_sems.at[n])
            )
            copies[-1].start()
        for copy in copies:
            copy.wait()

    @pl.when(jnp.logical_not(general))
    def _():
        copy = pltpu.make_async_copy(a, out, out_sems.at[0])
        copy.start()
        copy.wait()


def shards(matrix, pivot_inv, pattern):
    f32, bf16 = jnp.float32, jnp.bfloat16
    in_hbm, in_vmem = pl.BlockSpec(memory_space=pltpu.HBM), pl.BlockSpec(memory_space=pltpu.VMEM)
    parts = pl.pallas_call(
        kernel,
        out_shape=[pltpu.VMEM(matrix.shape, f32)]
        + [pltpu.VMEM((1024, 512), bf16)] * 2
        + [pltpu.VMEM((512, 1024), bf16)] * 2,
        in_specs=[in_hbm] * 3,
        out_specs=[in_vmem] * 5,
        scratch_shapes=[
            pltpu.VMEM((TICKS_L, 4, 2, B // R, B), f32),
            pltpu.VMEM((64, 2, B // 2, B), f32),
            pltpu.VMEM(pivot_inv.shape, f32),
            pltpu.SMEM(pattern.shape, jnp.int32),
            pltpu.SemaphoreType.DMA((64 * R,)),
            pltpu.SemaphoreType.DMA((16 * R,)),
            pltpu.SemaphoreType.DMA((64 * R,)),
            pltpu.SemaphoreType.DMA((128,)),
            pltpu.SemaphoreType.DMA((4,)),
            pltpu.SemaphoreType.DMA((4,)),
            pltpu.SemaphoreType.DMA,
            pltpu.SemaphoreType.DMA((2,)),
            pltpu.SemaphoreType.DMA,
            pltpu.SemaphoreType.DMA((10,)),
        ],
        compiler_params=pltpu.CompilerParams(
            collective_id=0, has_side_effects=True, vmem_limit_bytes=50 << 20
        ),
        cost_estimate=pl.CostEstimate(
            flops=5 * 1024**3, bytes_accessed=8 << 20, transcendentals=0
        ),
        name="factor",
    )(matrix, pivot_inv, pattern)
    return pl.pallas_call(
        finish,
        out_shape=jax.ShapeDtypeStruct(matrix.shape, f32),
        in_specs=[in_vmem] * 5 + [in_hbm],
        out_specs=in_hbm,
        scratch_shapes=[
            pltpu.VMEM((1024, 1024), f32),
            pltpu.SMEM(pattern.shape, jnp.int32),
            pltpu.SemaphoreType.DMA,
            pltpu.SemaphoreType.DMA((4,)),
        ],
        compiler_params=pltpu.CompilerParams(vmem_limit_bytes=12 << 20),
        cost_estimate=pl.CostEstimate(
            flops=3 * 512 * 1024**2, bytes_accessed=8 << 20, transcendentals=0
        ),
        name="finish",
    )(*parts, pattern)


def solution(mesh):
    return jax.shard_map(
        shards,
        mesh=mesh,
        in_specs=(P("prow", "pcol"), P(), P("prow", "pcol")),
        out_specs=P("prow", "pcol"),
        check_vma=False,
    )
```
